128 devices in a mesh: dp: 8 (over y, x_hi), expert: 16 (over z, x_lo, core).
Axes of the slice: x: 4 (x_hi: 2, x_lo: 2; x = x_hi * 2 + x_lo), y: 4, z: 4, core: 2. Of those that a mesh axis runs over, the one named last changes fastest.
Arguments:
- tokens: bfloat16 [4096, 2048], P('expert'), may hold values from -6 to 6
- out_grad: bfloat16 [4096, 2048], P('expert'), may hold values from -2 to 2
- expert_ids: int32 [4096, 2], P('expert'), may hold values from 0 to 15, all different within a row; in each aligned block of 256 rows (0 to 255, 256 to 511, ...) at most 64 rows name the same one
- gate_probs: bfloat16 [4096, 2], P('expert'), may hold values from 0.099609375 to 1
- w_gate: bfloat16 [16, 768, 2048], P('expert', 'dp'), may hold values from -0.125 to 0.125
- w_up: bfloat16 [16, 768, 2048], P('expert', 'dp'), may hold values from -0.125 to 0.125
- w_down: bfloat16 [16, 768, 2048], P('expert', 'dp'), may hold values from -0.21875 to 0.21875
Outputs:
- token_grad: float32 [4096, 2048], P('expert', 'dp')
- prob_grad: float32 [4096, 2], P('expert')
- grad_gate: float32 [16, 768, 2048], P('expert', 'dp')
- grad_up: float32 [16, 768, 2048], P('expert', 'dp')
- grad_down: float32 [16, 768, 2048], P('expert', 'dp')
The draws below stay inside these ranges and needn't reach their ends.
Inputs may be any that keep to these rules, and one draw needn't show every extreme that they name: `expert_ids`: in the rows of one device no expert is named by more than 64 rows; the 2 experts of a token differ.
All inputs are finite; a program needn't handle non-finite values.
Results may differ from the reference program's by a relative error of at most 0.02.
Values may be sent and summed in bfloat16 or wider, within the bound.
A program may use at most 128 MiB of HBM per device.

```python
import math
import jax
import jax.numpy as jnp
import numpy as np
from jax import lax

D = 2048
FF = 768
TOP = 2
TOK_DEV = 256
EXPERTS = 16
TOKENS = 4096
CAP = 64
N_EXPERT = 16


def shard_levels(rng, extent, pieces, least, largest):
    def one(dim, shards_of):
        heights = jax.random.uniform(jax.random.fold_in(jax.random.fold_in(rng, 6), dim), (shards_of,), jnp.float32, least / len(pieces), largest / len(pieces))
        return jnp.repeat(jnp.exp(heights), extent[dim] // shards_of).reshape((-1,) + (1,) * (len(extent) - dim - 1))

    loudness = one(*pieces[0])
    for cut in pieces[1:]:
        loudness = loudness * one(*cut)
    return loudness


def shared_out(own_key, own, number, rows, number_of, top, reach, skew):
    order = jax.random.permutation(own_key, number_of)
    crowded, ordinary = portions_of(number_of, rows * top, reach, skew, True), portions_of(number_of, rows * top, reach, skew, False)
    places = jnp.arange(number_of)

    def named(lengths, offset_by):
        used = int((lengths > 0).sum())
        fixed = max(1, used // 4)
        moved = fixed + (places - fixed + offset_by * (used - fixed)) % max(1, number_of - fixed)
        return jnp.zeros((number_of,), jnp.int32).at[order[jnp.where(places < fixed, places, moved)]].set(jnp.asarray(lengths, jnp.int32))

    lengths = jnp.where(number % 4 == 0, named(crowded, number // 4), named(ordinary, number - number // 4 - 1))
    mixed = jax.random.permutation(jax.random.fold_in(own, 3), number_of)
    donor, sink = mixed[0:number_of // 2 * 2:2], mixed[1:number_of // 2 * 2:2]
    margin = jnp.minimum(lengths[donor] - 1, reach - lengths[sink]) // 2
    margin = jnp.where((donor == order[0]) | (sink == order[0]) | (lengths[sink] == 0), 0, jnp.maximum(margin, 0))
    moved = jax.random.randint(jax.random.fold_in(own, 4), (number_of // 2,), 0, 1 << 20) % (margin + 1)
    lengths = lengths.at[donor].add(-moved).at[sink].add(moved)
    items = jnp.searchsorted(jnp.cumsum(lengths), jnp.arange(rows * top), side="right").astype(jnp.int32)
    grid = items.reshape(top, rows).T
    grid = grid[jax.random.permutation(jax.random.fold_in(own, 1), rows)]
    offset_by = jax.random.randint(jax.random.fold_in(own, 2), (rows, 1), 0, top)
    return jnp.take_along_axis(grid, (jnp.arange(top)[None, :] + offset_by) % top, axis=1)


def portions_of(amount, total, reach, skew, full):
    portions = [(1 << 20) // math.isqrt(grade ** skew) + 1 for grade in range(1, amount + 1)]
    largest = reach if full else min(reach, max(-(-total // amount), total * portions[0] // sum(portions)))
    least = 1 if total - largest >= amount - 1 else 0
    holding, rest = [largest] + [least] * (amount - 1), total - largest - least * (amount - 1)
    while rest > 0:
        candidates = [i for i in range(1, amount) if holding[i] < largest] or [i for i in range(1, amount) if holding[i] < reach]
        whole, budget = sum([portions[i] for i in candidates]), rest
        for i in candidates:
            more = min(reach - holding[i], max(1, budget * portions[i] // whole), rest)
            holding[i] = holding[i] + more
            rest = rest - more
    return np.array(holding)


def noise(stream_key, extent, width, limit, cuts=(), kind=jnp.bfloat16):
    array = jax.random.normal(stream_key, extent, jnp.float32) * width
    if len(cuts) > 0:
        array = shard_levels(stream_key, extent, cuts, -0.22, 0.18) * array
    return jnp.clip(array, min=-limit, max=limit).astype(kind)


def setup_inputs(seed: int = 0) -> dict:
    arg_keys = jax.random.split(jax.random.key(seed), 8)
    tokens = noise(arg_keys[0], (TOKENS, D), 1.0, 6.0, ((0, 16),))
    out_grad = noise(arg_keys[1], (TOKENS, D), 0.3, 2.0, ((0, 16),))
    expert_ids_keys = jax.random.split(jax.random.fold_in(arg_keys[2], 1), TOKENS // TOK_DEV)
    expert_ids_turns = jax.random.permutation(jax.random.fold_in(arg_keys[2], 3), TOKENS // TOK_DEV)
    expert_ids = jax.vmap(lambda own, number: shared_out(jax.random.fold_in(arg_keys[2], 2), own, number, TOK_DEV, EXPERTS, TOP, CAP, 2))(expert_ids_keys, expert_ids_turns).reshape((TOKENS, TOP))
    gate_probs = jnp.clip(0.099609375 + 0.9003906 * jax.random.uniform(arg_keys[3], (TOKENS, TOP), jnp.float32) ** shard_levels(arg_keys[3], (TOKENS, TOP), ((0, 16),), -0.2, 0.2), 0.099609375, 1.0).astype(jnp.bfloat16)
    w_gate = noise(arg_keys[4], (EXPERTS, FF, D), D ** -0.5, 0.125, ((0, 16), (1, 8)))
    w_up = noise(arg_keys[5], (EXPERTS, FF, D), D ** -0.5, 0.125, ((0, 16), (1, 8)))
    w_down = noise(arg_keys[6], (EXPERTS, FF, D), FF ** -0.5, 0.21875, ((0, 16), (1, 8)))
    return dict(tokens=tokens, out_grad=out_grad, expert_ids=expert_ids, gate_probs=gate_probs, w_gate=w_gate, w_up=w_up, w_down=w_down)


def slot_tables(expert_ids, experts, capacity):
    tokens, routes = expert_ids.shape
    flattened = expert_ids.reshape(-1)
    one_hot = (flattened[:, None] == jnp.arange(experts, dtype=jnp.int32)[None, :]).astype(jnp.int32)
    earlier = jnp.cumsum(one_hot, axis=0) - one_hot
    position = jnp.sum(earlier * one_hot, axis=1)
    target = (flattened * capacity + position).astype(jnp.int32)
    serial = jnp.arange(tokens * routes, dtype=jnp.int32)
    slot_index = jnp.zeros((experts * capacity,), jnp.int32).at[target].set(serial).reshape(experts, capacity)
    filled = jnp.zeros((experts * capacity,), jnp.float32).at[target].set(1.0).reshape(experts, capacity)
    return slot_index, filled


def rounded(values):
    return lax.optimization_barrier(values.astype(jnp.bfloat16)).astype(jnp.float32)


def expert_math(slot_x, slot_dy, slot_p, weight_gate, weight_up, weight_down):
    gate_pre = jnp.einsum("ecd,efd->ecf", slot_x, weight_gate)
    up_pre = jnp.einsum("ecd,efd->ecf", slot_x, weight_up)
    sigmoid_gate = jax.nn.sigmoid(gate_pre)
    active = gate_pre * sigmoid_gate
    hidden = active * up_pre
    hidden_low = rounded(hidden)
    backed = jnp.einsum("ecd,efd->ecf", slot_dy, weight_down)
    prob_slot = jnp.sum(hidden * backed, axis=-1)
    prob_column = slot_p[..., None]
    grad_hidden = prob_column * backed
    grad_gate_pre = rounded(grad_hidden * up_pre * sigmoid_gate * (1.0 + gate_pre * (1.0 - sigmoid_gate)))
    grad_up_pre = rounded(grad_hidden * active)
    scaled = rounded(prob_column * slot_dy)
    dx_slot = jnp.einsum("ecf,efd->ecd", grad_gate_pre, weight_gate) + jnp.einsum("ecf,efd->ecd", grad_up_pre, weight_up)
    partial_gate = jnp.einsum("ecf,ecd->efd", grad_gate_pre, slot_x)
    partial_up = jnp.einsum("ecf,ecd->efd", grad_up_pre, slot_x)
    partial_down = jnp.einsum("ecf,ecd->efd", hidden_low, scaled)
    return dx_slot, prob_slot, (partial_gate, partial_up, partial_down)


def reference(tokens, out_grad, expert_ids, gate_probs, w_gate, w_up, w_down):
    weight_gate = w_gate.astype(jnp.float32)
    weight_up = w_up.astype(jnp.float32)
    weight_down = w_down.astype(jnp.float32)
    blocks = N_EXPERT
    block_x = tokens.reshape(blocks, TOK_DEV, D)
    block_dy = out_grad.reshape(blocks, TOK_DEV, D)
    block_ids = expert_ids.reshape(blocks, TOK_DEV, TOP)
    block_p = gate_probs.reshape(blocks, TOK_DEV, TOP)

    def per_block(totals, inputs):
        this_x, this_dy, this_ids, this_p = inputs
        slot_index, filled = slot_tables(this_ids, EXPERTS, CAP)
        token_row = slot_index // TOP
        slot_x = this_x[token_row].astype(jnp.float32)
        slot_dy = this_dy[token_row].astype(jnp.float32)
        slot_p = (this_p.reshape(-1)[slot_index] * filled.astype(jnp.bfloat16)).astype(jnp.float32)
        dx_slot, prob_slot, partials = expert_math(slot_x, slot_dy, slot_p, weight_gate, weight_up, weight_down)
        new_totals = tuple(total + rounded(term) for total, term in zip(totals, partials))
        dx_rows = jnp.zeros((TOK_DEV, D), jnp.float32).at[token_row.reshape(-1)].add((dx_slot * filled[..., None]).reshape(-1, D))
        prob_rows = jnp.zeros((TOK_DEV * TOP,), jnp.float32).at[slot_index.reshape(-1)].add((prob_slot * filled).reshape(-1))
        return new_totals, (dx_rows, prob_rows.reshape(TOK_DEV, TOP))

    zeros_grad = jnp.zeros((EXPERTS, FF, D), jnp.float32)
    totals, outputs = lax.scan(per_block, (zeros_grad, zeros_grad, zeros_grad), (block_x, block_dy, block_ids, block_p))
    dx_all, prob_all = outputs
    return dx_all.reshape(TOKENS, D), prob_all.reshape(TOKENS, TOP), totals[0], totals[1], totals[2]
```

```python
import jax
import jax.numpy as jnp
from jax import lax
from jax.experimental import pallas as pl
from jax.experimental.pallas import tpu as pltpu
from jax.sharding import PartitionSpec as P

MESH = pl.DeviceIdType.MESH
F32 = jnp.float32
BF16 = jnp.bfloat16

D = 2048
FF = 96
TOK = 256
CAP = 64
Q = 512
ROWS = 8 * CAP
HALF = ROWS // 2


def dot(a, b):
    return jnp.dot(a, b, preferred_element_type=F32)


def dot_nt(a, b):
    return lax.dot_general(a, b, (((1,), (1,)), ((), ())), preferred_element_type=F32)


def dot_tn(a, b):
    return lax.dot_general(a, b, (((0,), (0,)), ((), ())), preferred_element_type=F32)


def kernel(
    tok,
    dy,
    meta,
    wg,
    wu,
    wd,
    o_tok,
    o_prob,
    o_g,
    o_u,
    o_d,
    mb,
    xo,
    raw,
    stage,
    slots,
    wgu,
    wdn,
    upper,
    p_own,
    p_oth,
    pcol,
    pre,
    bk,
    ga,
    hl,
    scaled,
    dsend,
    drecv,
    dback,
    down,
    pb,
    po,
    pf,
    gsend,
    grecv,
    tsend,
    trecv,
    l_sem,
    m_s,
    m_r,
    raw_s,
    raw_r,
    w_s,
    w_r,
    d_s,
    d_r,
    f_s,
    f_r,
    x_s,
    x_r,
    pb_s,
    pb_r,
    rb_s,
    rb_r,
    g_s,
    g_r,
    t_s,
    t_r,
    pf_s,
    pf_r,
):
    dp = lax.axis_index("dp")
    ex = lax.axis_index("expert")
    y, h = dp // 2, dp % 2
    z, l, c = ex // 4, (ex // 2) % 2, ex % 2
    active = c == h
    base = (y % 2) * 2

    def device(yy, hh, zz, ll, cc):
        return (((yy + 4) % 4) * 2 + hh, ((zz + 4) % 4) * 4 + ll * 2 + cc)

    def remote(src, dst, send, recv, target):
        return pltpu.make_async_remote_copy(
            src_ref=src,
            dst_ref=dst,
            send_sem=send,
            recv_sem=recv,
            device_id=target,
            device_id_type=MESH,
        )

    here = (dp, ex)

    barrier = pltpu.get_barrier_semaphore()
    for n in range(1, 16):
        pl.semaphore_signal(barrier, inc=1, device_id=(dp, (ex + n) % 16), device_id_type=MESH)
    for n in range(1, 8):
        pl.semaphore_signal(barrier, inc=1, device_id=((dp + n) % 8, ex), device_id_type=MESH)

    local = [
        pltpu.make_async_copy(wg.at[0], wgu.at[0, pl.ds(0, FF)], l_sem.at[0]),
        pltpu.make_async_copy(wu.at[0], wgu.at[0, pl.ds(128, FF)], l_sem.at[1]),
        pltpu.make_async_copy(wd.at[0], wdn.at[0, pl.ds(0, FF)], l_sem.at[2]),
    ]
    for copy in local:
        copy.start()

    def quarter_of(ref, q):
        return ref.at[:, pl.ds(pl.multiple_of((base + q) * Q, Q), Q)]

    own_copies = [
        pltpu.make_async_copy(quarter_of(ref, q), xo.at[q, :, pl.ds(i * Q, Q)], l_sem.at[3 + 2 * q + i])
        for q in range(2)
        for i, ref in enumerate((tok, dy))
    ]

    @pl.when(active)
    def _():
        for copy in own_copies:
            copy.start()

    zeros = jnp.zeros((128 - FF, D), BF16)
    for j in range(2):
        wgu[j, FF:128] = zeros
        wgu[j, 128 + FF : 256] = zeros
        wdn[j, FF:128] = zeros
    upper[...] = (
        lax.broadcasted_iota(jnp.int32, (TOK, TOK), 0) < lax.broadcasted_iota(jnp.int32, (TOK, TOK), 1)
    ).astype(F32).astype(BF16)
    slot_iota = lax.broadcasted_iota(jnp.int32, (CAP, TOK), 0).astype(F32)
    eye = (
        lax.broadcasted_iota(jnp.int32, (CAP, 128), 0) == lax.broadcasted_iota(jnp.int32, (CAP, 128), 1)
    ).astype(F32)

    def targets(named):
        before = dot(named.astype(BF16), upper[...])
        return jnp.where(named > 0, before, -1.0)

    def one_hot(target_row):
        return (slot_iota == target_row).astype(F32)

    pl.semaphore_wait(barrier, 22)

    def raw_copy(q, i):
        ref = (tok, dy)[i]
        return remote(
            quarter_of(ref, q),
            raw.at[q, :, pl.ds(i * Q, Q)],
            raw_s.at[2 * q + i],
            raw_r.at[2 * q + i],
            device(y, h, z, 1 - l, c),
        )

    def meta_copy(w, k, cc):
        n = (w * 4 + k) * 2
        return remote(
            meta,
            mb.at[w * 4 + k],
            m_s.at[n + cc],
            m_r.at[w * 4 + k],
            device(y, h, z + k, l if w == 0 else 1 - l, cc),
        )

    def each_peer(w, k, f):
        for cc in range(2):
            if w == 0 and k == 0:

                @pl.when(cc != c)
                def _(cc=cc):
                    f(cc)

            else:
                f(cc)

    def w_copy(n):
        src = (wg, wu, wd)[n]
        dst = (wgu.at[1, pl.ds(0, FF)], wgu.at[1, pl.ds(128, FF)], wdn.at[1, pl.ds(0, FF)])[n]
        return remote(src.at[0], dst, w_s.at[n], w_r.at[n], device(y, 1 - h, z, l, c))

    @pl.when(active)
    def _():
        for w in range(2):
            for k in range(4):
                each_peer(w, k, lambda cc, w=w, k=k: meta_copy(w, k, cc).start())
        for q in range(2):
            for i in range(2):
                raw_copy(q, i).start()

    for n in range(3):
        w_copy(n).start()

    def d_copy(w, k, cc, q):
        n = (w * 4 + k) * 2
        return remote(
            stage.at[w, q, pl.ds((k * 2 + cc) * CAP, CAP)],
            slots.at[base + q, pl.ds((w * 4 + k) * CAP, CAP)],
            d_s.at[(n + cc) * 2 + q],
            d_r.at[n + q],
            device(y, h, z + k, l, cc),
        )

    def f_copy(s, q):
        rows = slots.at[base + q, pl.ds(s * CAP, CAP)]
        return remote(
            rows, rows, f_s.at[2 * s + q], f_r.at[2 * s + q], device(y + (-1 if q == 0 else 1), h, z, l, c)
        )

    def f_wait(s, q):
        rows = slots.at[2 - base + q, pl.ds(s * CAP, CAP)]
        remote(
            rows, rows, f_s.at[2 * s + q], f_r.at[2 * s + q], device(y + (1 if q == 0 else -1), h, z, l, c)
        ).wait_recv()

    order = (1, 3, 2, 0)

    def named_by(ids0, ids1, experts):
        first = (ids0 == experts).astype(F32)
        second = (ids1 == experts).astype(F32)
        return first, second

    def expert_column(count, w0):
        r = lax.broadcasted_iota(jnp.int32, (count, 1), 0) + w0 * 8
        return (4 * ((z + (r // 2) % 4) % 4) + 2 * ((l + r // 8) % 2) + r % 2).astype(F32)

    def dispatch(w, source, chooser):
        for q in range(2):
            stage[w, q] = dot(chooser[0:ROWS, :], source[q]).astype(BF16)
            for k in order:

                def send(cc, k=k, q=q):
                    d_copy(w, k, cc, q).start()

                if k == 0:
                    for cc in range(2):

                        @pl.when(cc != c)
                        def _(cc=cc):
                            send(cc)

                else:
                    for cc in range(2):
                        send(cc)
            slots[base + q, w * 4 * CAP : w * 4 * CAP + CAP] = stage[
                w, q, pl.ds(pl.multiple_of(c * CAP, CAP), CAP)
            ]

    @pl.when(active)
    def _():
        mb[0] = meta[...]
        first, second = named_by(meta[0:1], meta[1:2], expert_column(16, 0))
        where = targets(first + second)
        for r in range(16):
            p_own[r * CAP : (r + 1) * CAP] = one_hot(where[r : r + 1]).astype(BF16)
        for copy in own_copies:
            copy.wait()
        dispatch(0, xo, p_own)
        for q in range(2):
            f_copy(0, q).start()
        meta_copy(1, 0, 0).wait_recv()
        for q in range(2):
            for i in range(2):
                raw_copy(q, i).wait_recv()
        theirs = mb[4]
        first, second = named_by(theirs[0:1], theirs[1:2], expert_column(8, 0))
        where = targets(first + second)
        for r in range(8):
            p_oth[r * CAP : (r + 1) * CAP] = one_hot(where[r : r + 1]).astype(BF16)
        dispatch(1, raw, p_oth)
        for q in range(2):
            f_copy(4, q).start()

    for w in range(2):
        for k in order:
            s = w * 4 + k

            def arrive(w=w, k=k, s=s):
                for q in range(2):
                    d_copy(w, k, 0, q).wait_recv()
                    f_copy(s, q).start()

            if k == 0:
                pl.when(jnp.logical_not(active))(arrive)
            else:
                arrive()

    @pl.when(jnp.logical_not(active))
    def _():
        meta_copy(0, 0, 0).wait_recv()
        meta_copy(1, 0, 0).wait_recv()

    for s in (1, 2, 3, 5, 6, 7):
        meta_copy(s // 4, s % 4, 0).wait_recv()
    mine = jnp.full((1, 1), ex, jnp.int32).astype(F32)
    firsts, seconds = named_by(mb[:, 0, :], mb[:, 1, :], mine)
    where = targets(firsts + seconds)
    weight = firsts * mb[:, 2, :] + seconds * mb[:, 3, :]
    for s in range(8):
        chosen = one_hot(where[s : s + 1]) * weight[s : s + 1]
        column = jnp.sum(chosen, axis=1, keepdims=True)
        pcol[s * CAP : (s + 1) * CAP] = jnp.broadcast_to(column, (CAP, 128))

    for copy in local:
        copy.wait()

    def inward(j, w):
        rows = slice(w * HALF, (w + 1) * HALF)
        acc_gu = jnp.zeros((HALF, 256), F32)
        acc_d = jnp.zeros((HALF, 128), F32)
        for q in range(4):
            acc_gu += dot_nt(slots[q, rows, 0:Q], wgu[j, :, q * Q : (q + 1) * Q])
            acc_d += dot_nt(slots[q, rows, Q : 2 * Q], wdn[j, :, q * Q : (q + 1) * Q])
        pre[j, rows] = acc_gu
        bk[j, rows] = acc_d

    for w in range(2):
        for k in order:
            for q in range(2):
                f_wait(w * 4 + k, q)
        rows = slice(w * HALF, (w + 1) * HALF)
        for q in range(4):
            scaled[q, rows] = (slots[q, rows, Q : 2 * Q].astype(F32) * pcol[rows, 0:1]).astype(BF16)
        inward(0, w)

    for n in range(3):
        w_copy(n).wait_recv()

    def x_copy(w, n):
        step = (1, -1, 2)[n]
        rows = pl.ds(w * HALF, HALF)
        return remote(
            dsend.at[(y + step + 4) % 4, rows],
            drecv.at[(1, 0, 2)[n], rows],
            x_s.at[w * 3 + n],
            x_r.at[w * 3 + (1, 0, 2)[n]],
            device(y + step, h, z, l, c),
        )

    def pb_copy(w, k):
        s = w * 4 + k
        r = w * 8 + k * 2 + c
        return remote(
            pb.at[s], po.at[r], pb_s.at[s], pb_r.at[r], device(y, h, z - k, l if w == 0 else 1 - l, h)
        )

    for w in range(2):
        inward(1, w)
        for half in range(2):
            rows = slice(w * HALF + half * 128, w * HALF + half * 128 + 128)
            total = jnp.zeros((128, 128), F32)
            for j in range(2):
                gate = pre[j, rows, 0:128]
                up = pre[j, rows, 128:256]
                backed = bk[j, rows]
                sig = jax.nn.sigmoid(gate)
                act = gate * sig
                hidden = act * up
                total += hidden * backed
                back = backed * pcol[rows]
                ga[j, rows, 0:128] = (back * up * sig * (1.0 + gate * (1.0 - sig))).astype(BF16)
                ga[j, rows, 128:256] = (back * act).astype(BF16)
                hl[j, rows] = hidden.astype(BF16)
            column = jnp.sum(total, axis=1, keepdims=True)
            for n in range(2):
                s = w * 4 + half * 2 + n
                row = jnp.sum(eye * column[n * CAP : (n + 1) * CAP], axis=0, keepdims=True)
                pb[s] = jnp.broadcast_to(row, (8, 128))
        rows = slice(w * HALF, (w + 1) * HALF)
        for q in range(4):
            part = dot(ga[0, rows], wgu[0, :, q * Q : (q + 1) * Q]) + dot(
                ga[1, rows], wgu[1, :, q * Q : (q + 1) * Q]
            )
            dsend[q, rows] = part.astype(BF16)
        for n in range(3):
            x_copy(w, n).start()
        for k in order:
            if w == 0 and k == 0:
                pl.when(jnp.logical_not(active))(lambda: pb_copy(0, 0).start())
            else:
                pb_copy(w, k).start()

    def g_copy(q):
        return remote(gsend.at[q], grecv.at[q], g_s.at[q], g_r.at[q], device(y, 1 - h, z, l, c))

    for q in range(4):
        part = dot_tn(ga[1], slots[q, :, 0:Q]).astype(BF16)
        gsend[q, 0] = part[0:FF]
        gsend[q, 1] = part[128 : 128 + FF]
        gsend[q, 2] = dot_tn(hl[1], scaled[q]).astype(BF16)[0:FF]
        g_copy(q).start()
    for q in range(4):
        lanes = slice(q * Q, (q + 1) * Q)
        part = dot_tn(ga[0], slots[q, :, 0:Q])
        o_g[0, :, lanes] = part[0:FF]
        o_u[0, :, lanes] = part[128 : 128 + FF]
        o_d[0, :, lanes] = dot_tn(hl[0], scaled[q])[0:FF]

    def rb_copy(w, k):
        s = w * 4 + k
        r = w * 8 + k * 2 + c
        return remote(
            dback.at[pl.ds(s * CAP, CAP)],
            down.at[pl.ds(pl.multiple_of(r * CAP, CAP), CAP)],
            rb_s.at[s],
            rb_r.at[r],
            device(y, h, z - k, l if w == 0 else 1 - l, h),
        )

    for w in range(2):
        for n in range(3):
            x_copy(w, n).wait_recv()
        rows = slice(w * HALF, (w + 1) * HALF)
        total = dsend[y, rows].astype(F32)
        for n in range(3):
            total += drecv[n, rows].astype(F32)
        dback[rows] = total.astype(BF16)
        for k in order:
            if w == 0 and k == 0:
                pl.when(jnp.logical_not(active))(lambda: rb_copy(0, 0).start())
            else:
                rb_copy(w, k).start()

    def pf_copy(n):
        step, hh = n % 4, n // 4
        return remote(
            pf.at[0],
            pf.at[(4 - step) % 4 if n != 4 else 0],
            pf_s.at[n],
            pf_r.at[(4 - step) % 4],
            device(y + step, h if hh == 0 else 1 - h, z, l, c),
        )

    def t_copy():
        return remote(tsend, trecv, t_s.at[0], t_r.at[0], device(y, 1 - h, z, l, c))

    def owner_recv(copy):
        for w in range(2):
            for k in range(4):
                for cc in range(2):
                    r = w * 8 + k * 2 + cc

                    def wait(r=r):
                        copy(r).wait_recv()

                    if w == 0 and k == 0:
                        pl.when(cc != c)(wait)
                    else:
                        wait()

    @pl.when(active)
    def _():
        po[c] = pb[0]
        owner_recv(lambda r: remote(pb.at[0], po.at[r], pb_s.at[0], pb_r.at[r], device(y, 1 - h, z, l, c)))
        first, second = named_by(meta[0:1], meta[1:2], expert_column(16, 0))
        sums = [jnp.zeros((1, TOK), F32), jnp.zeros((1, TOK), F32)]
        for r in range(16):
            column = jnp.sum(eye * po[r, 0:1, :], axis=1, keepdims=True)
            row = jnp.sum(p_own[r * CAP : (r + 1) * CAP].astype(F32) * column, axis=0, keepdims=True)
            sums[0] += row * first[r : r + 1]
            sums[1] += row * second[r : r + 1]
        pf[0] = jnp.concatenate(sums + [jnp.zeros((6, TOK), F32)], axis=0)
        for n in range(1, 8):
            pf_copy(n).start()
        down[pl.ds(pl.multiple_of(c * CAP, CAP), CAP)] = dback[0:CAP]
        owner_recv(
            lambda r: remote(
                dback.at[pl.ds(0, CAP)],
                down.at[pl.ds(r * CAP, CAP)],
                rb_s.at[0],
                rb_r.at[r],
                device(y, 1 - h, z, l, c),
            )
        )
        grad = dot_tn(p_own[...], down[...])
        near, far = grad[:, 0:256], grad[:, 256:512]
        low = h == 0
        tsend[...] = jnp.where(low, far, near).astype(BF16)
        t_copy().start()
        o_tok[...] = jnp.where(low, near, far)

    @pl.when(jnp.logical_not(active))
    def _():
        t_copy().wait_recv()
        o_tok[...] = trecv[...].astype(F32)
        pf_copy(4).wait_recv()

    for n in (1, 2, 3):
        remote(pf.at[0], pf.at[n], pf_s.at[n], pf_r.at[n], device(y + n, h, z, l, c)).wait_recv()
    o_prob[...] = pf[0] + pf[1] + pf[2] + pf[3]

    for q in range(4):
        g_copy(q).wait_recv()
        lanes = slice(q * Q, (q + 1) * Q)
        for n, out in enumerate((o_g, o_u, o_d)):
            out[0, :, lanes] = out[0, :, lanes] + grecv[q, n].astype(F32)

    @pl.when(active)
    def _():
        for w in range(2):
            for k in range(4):
                each_peer(w, k, lambda cc, w=w, k=k: meta_copy(w, k, cc).wait_send())
                for q in range(2):
                    for cc in range(2):
                        if k == 0:
                            pl.when(cc != c)(lambda w=w, k=k, cc=cc, q=q: d_copy(w, k, cc, q).wait_send())
                        else:
                            d_copy(w, k, cc, q).wait_send()
        for q in range(2):
            for i in range(2):
                raw_copy(q, i).wait_send()
        for n in range(1, 8):
            pf_copy(n).wait_send()
        t_copy().wait_send()

    for n in range(3):
        w_copy(n).wait_send()
    for s in range(8):
        for q in range(2):
            f_copy(s, q).wait_send()
    for w in range(2):
        for n in range(3):
            x_copy(w, n).wait_send()
        for k in range(4):

            def sent(w=w, k=k):
                pb_copy(w, k).wait_send()
                rb_copy(w, k).wait_send()

            if w == 0 and k == 0:
                pl.when(jnp.logical_not(active))(sent)
            else:
                sent()
    for q in range(4):
        g_copy(q).wait_send()


def on_device(tokens, out_grad, expert_ids, gate_probs, w_gate, w_up, w_down):
    meta = jnp.concatenate(
        [expert_ids.T.astype(F32), gate_probs.T.astype(F32), jnp.zeros((4, TOK), F32)], axis=0
    )
    dma = pltpu.SemaphoreType.DMA
    anywhere = pl.BlockSpec(memory_space=pl.ANY)
    vmem = pl.BlockSpec(memory_space=pltpu.VMEM)
    token_grad, prob, grad_gate, grad_up, grad_down = pl.pallas_call(
        kernel,
        out_shape=(
            jax.ShapeDtypeStruct((TOK, 256), F32),
            jax.ShapeDtypeStruct((8, TOK), F32),
            jax.ShapeDtypeStruct((1, FF, D), F32),
            jax.ShapeDtypeStruct((1, FF, D), F32),
            jax.ShapeDtypeStruct((1, FF, D), F32),
        ),
        in_specs=[anywhere, anywhere, vmem, anywhere, anywhere, anywhere],
        out_specs=(vmem,) * 5,
        scratch_shapes=[
            pltpu.VMEM((8, 8, TOK), F32),
            pltpu.VMEM((2, TOK, 2 * Q), BF16),
            pltpu.VMEM((2, TOK, 2 * Q), BF16),
            pltpu.VMEM((2, 2, ROWS, 2 * Q), BF16),
            pltpu.VMEM((4, ROWS, 2 * Q), BF16),
            pltpu.VMEM((2, 256, D), BF16),
            pltpu.VMEM((2, 128, D), BF16),
            pltpu.VMEM((TOK, TOK), BF16),
            pltpu.VMEM((16 * CAP, TOK), BF16),
            pltpu.VMEM((8 * CAP, TOK), BF16),
            pltpu.VMEM((ROWS, 128), F32),
            pltpu.VMEM((2, ROWS, 256), F32),
            pltpu.VMEM((2, ROWS, 128), F32),
            pltpu.VMEM((2, ROWS, 256), BF16),
            pltpu.VMEM((2, ROWS, 128), BF16),
            pltpu.VMEM((4, ROWS, Q), BF16),
            pltpu.VMEM((4, ROWS, Q), BF16),
            pltpu.VMEM((3, ROWS, Q), BF16),
            pltpu.VMEM((ROWS, Q), BF16),
            pltpu.VMEM((16 * CAP, Q), BF16),
            pltpu.VMEM((8, 8, 128), F32),
            pltpu.VMEM((16, 8, 128), F32),
            pltpu.VMEM((4, 8, TOK), F32),
            pltpu.VMEM((4, 3, FF, Q), BF16),
            pltpu.VMEM((4, 3, FF, Q), BF16),
            pltpu.VMEM((TOK, 256), BF16),
            pltpu.VMEM((TOK, 256), BF16),
            dma((7,)),
            dma((16,)),
            dma((8,)),
            dma((4,)),
            dma((4,)),
            dma((3,)),
            dma((3,)),
            dma((32,)),
            dma((16,)),
            dma((16,)),
            dma((16,)),
            dma((6,)),
            dma((6,)),
            dma((8,)),
            dma((16,)),
            dma((8,)),
            dma((16,)),
            dma((4,)),
            dma((4,)),
            dma((1,)),
            dma((1,)),
            dma((8,)),
            dma((4,)),
        ],
        compiler_params=pltpu.CompilerParams(
            collective_id=0, has_side_effects=True, vmem_limit_bytes=48 << 20
        ),
        name="expert_backward",
    )(tokens, out_grad, meta, w_gate, w_up, w_down)
    return token_grad, prob[0:2].T, grad_gate, grad_up, grad_down


def solution(mesh):
    in_specs = (
        P("expert", None),
        P("expert", None),
        P("expert", None),
        P("expert", None),
        P("expert", "dp", None),
        P("expert", "dp", None),
        P("expert", "dp", None),
    )
    out_specs = (
        P("expert", "dp"),
        P("expert", None),
        P("expert", "dp", None),
        P("expert", "dp", None),
        P("expert", "dp", None),
    )
    return jax.shard_map(
        on_device, mesh=mesh, in_specs=in_specs, out_specs=out_specs, check_vma=False
    )
```

```python
import jax
import jax.numpy as jnp
from jax import lax
from jax.experimental import pallas as pl
from jax.experimental.pallas import tpu as pltpu
from jax.sharding import PartitionSpec as P

MESH = pl.DeviceIdType.MESH
F32 = jnp.float32
BF16 = jnp.bfloat16

D = 2048
FF = 96
TOK = 256
CAP = 64
Q = 512
ROWS = 8 * CAP
HALF = ROWS // 2


def dot(a, b):
    return jnp.dot(a, b, preferred_element_type=F32)


def dot_nt(a, b):
    return lax.dot_general(a, b, (((1,), (1,)), ((), ())), preferred_element_type=F32)


def dot_tn(a, b):
    return lax.dot_general(a, b, (((0,), (0,)), ((), ())), preferred_element_type=F32)


def kernel(
    tok,
    dy,
    ids,
    prob,
    wg,
    wu,
    wd,
    o_tok,
    o_prob,
    o_g,
    o_u,
    o_d,
    meta,
    mb,
    xo,
    raw,
    stage,
    stage_oth,
    slots,
    wgu,
    wdn,
    upper,
    p_own,
    p_back,
    p_oth,
    pcol,
    pre,
    bk,
    ga,
    ga_t,
    hl_t,
    psum,
    scaled,
    dacc,
    dsend,
    far,
    near,
    csend,
    chain,
    dback,
    down,
    pb,
    po,
    pf,
    gd_send,
    gd_recv,
    gsend,
    grecv,
    tsend,
    trecv,
    l_sem,
    m_s,
    m_r,
    raw_s,
    raw_r,
    w_s,
    w_r,
    d_s,
    d_r,
    f_s,
    f_r,
    e_s,
    e_r,
    v_s,
    v_r,
    far_s,
    far_r,
    near_s,
    near_r,
    ch_s,
    ch_r,
    pb_s,
    pb_r,
    rb_s,
    rb_r,
    gd_s,
    gd_r,
    g_s,
    g_r,
    t_s,
    t_r,
    pf_s,
    pf_r,
):
    dp = lax.axis_index("dp")
    ex = lax.axis_index("expert")
    y, h = dp // 2, dp % 2
    z, l, c = ex // 4, (ex // 2) % 2, ex % 2
    active = c == h
    idle = jnp.logical_not(active)
    base = (y % 2) * 2

    def device(yy, hh, zz, ll, cc):
        return (((yy + 4) % 4) * 2 + hh, ((zz + 4) % 4) * 4 + ll * 2 + cc)

    def remote(src, dst, send, recv, target):
        return pltpu.make_async_remote_copy(
            src_ref=src,
            dst_ref=dst,
            send_sem=send,
            recv_sem=recv,
            device_id=target,
            device_id_type=MESH,
        )

    def other(w):
        return l if w == 0 else 1 - l

    barrier = pltpu.get_barrier_semaphore()
    for n in range(1, 16):
        pl.semaphore_signal(barrier, inc=1, device_id=(dp, (ex + n) % 16), device_id_type=MESH)
    for n in range(1, 8):
        pl.semaphore_signal(barrier, inc=1, device_id=((dp + n) % 8, ex), device_id_type=MESH)

    local = [
        pltpu.make_async_copy(wg.at[0], wgu.at[0, pl.ds(0, FF)], l_sem.at[0]),
        pltpu.make_async_copy(wu.at[0], wgu.at[0, pl.ds(128, FF)], l_sem.at[1]),
        pltpu.make_async_copy(wd.at[0], wdn.at[0, pl.ds(0, FF)], l_sem.at[2]),
    ]

    def quarter_of(ref, q):
        return ref.at[:, pl.ds(pl.multiple_of((base + q) * Q, Q), Q)]

    own_copies = [
        pltpu.make_async_copy(quarter_of(ref, q), xo.at[q, :, pl.ds(i * Q, Q)], l_sem.at[3 + 2 * q + i])
        for q in range(2)
        for i, ref in enumerate((tok, dy))
    ]

    @pl.when(active)
    def _():
        for copy in own_copies:
            copy.start()

    for copy in local:
        copy.start()
    meta[...] = jnp.concatenate(
        [ids[...].astype(F32), prob[...].astype(F32), jnp.zeros((4, TOK), F32)], axis=0
    )
    zeros = jnp.zeros((128 - FF, D), BF16)
    for j in range(2):
        wgu[j, FF:128] = zeros
        wgu[j, 128 + FF : 256] = zeros
        wdn[j, FF:128] = zeros
    upper[...] = (
        lax.broadcasted_iota(jnp.int32, (TOK, TOK), 0) < lax.broadcasted_iota(jnp.int32, (TOK, TOK), 1)
    ).astype(F32).astype(BF16)
    slot_iota = lax.broadcasted_iota(jnp.int32, (CAP, TOK), 0).astype(F32)
    eye = (
        lax.broadcasted_iota(jnp.int32, (CAP, 128), 0) == lax.broadcasted_iota(jnp.int32, (CAP, 128), 1)
    ).astype(F32)

    def targets(named):
        before = dot(named.astype(BF16), upper[...])
        return jnp.where(named > 0, before, -1.0)

    def one_hot(target_row):
        return (slot_iota == target_row).astype(F32)

    def named_by(ids0, ids1, experts):
        return (ids0 == experts).astype(F32), (ids1 == experts).astype(F32)

    def expert_column(count):
        r = lax.broadcasted_iota(jnp.int32, (count, 1), 0)
        return (4 * ((z + (r // 2) % 4) % 4) + 2 * ((l + r // 8) % 2) + r % 2).astype(F32)

    @pl.when(active)
    def _():
        mb[0] = meta[...]
        first, second = named_by(meta[0:1], meta[1:2], expert_column(16))
        where = targets(first + second)
        for r in range(16):
            p_own[r * CAP : (r + 1) * CAP] = one_hot(where[r : r + 1]).astype(BF16)

    pl.semaphore_wait(barrier, 22)

    def raw_copy(i):
        return remote(
            (tok, dy)[i].at[:, pl.ds(pl.multiple_of(y * Q, Q), Q)],
            raw.at[:, pl.ds(i * Q, Q)],
            raw_s.at[i],
            raw_r.at[i],
            device(y, h, z, 1 - l, c),
        )

    def meta_copy(w, k, cc):
        n = (w * 4 + k) * 2
        return remote(
            meta, mb.at[w * 4 + k], m_s.at[n + cc], m_r.at[w * 4 + k], device(y, h, z + k, other(w), cc)
        )

    def w_copy(n):
        src = (wg, wu, wd)[n]
        dst = (wgu.at[1, pl.ds(0, FF)], wgu.at[1, pl.ds(128, FF)], wdn.at[1, pl.ds(0, FF)])[n]
        return remote(src.at[0], dst, w_s.at[n], w_r.at[n], device(y, 1 - h, z, l, c))

    def each_peer(k, f):
        for cc in range(2):
            if k == 0:
                pl.when(cc != c)(lambda cc=cc: f(cc))
            else:
                f(cc)

    def each_meta(f):
        for w in range(2):
            for k in range(4):
                each_peer(k if w == 0 else 4, lambda cc, w=w, k=k: f(meta_copy(w, k, cc)))

    order = (1, 3, 2)

    def d_copy(w, k, cc, q):
        n = w * 16 + (k * 2 + cc) * 2 + q
        m = w * 8 + k * 2 + q
        rows = pl.ds((k * 2 + cc) * CAP, CAP)
        into = pl.ds((w * 4 + k) * CAP, CAP)
        return remote(
            stage.at[q, rows] if w == 0 else stage_oth.at[q, rows],
            slots.at[base + q, into] if w == 0 else slots.at[y, into, pl.ds(q * Q, Q)],
            d_s.at[n],
            d_r.at[m],
            device(y, h, z + k, l, cc),
        )

    def f_rows(k, q, up, quarter):
        return slots.at[quarter, pl.ds(k * CAP + 32 * ((up + q + 1) % 2), 32)]

    def f_copy(k, q, up):
        n = (2 * k + q) * 2 + up
        rows = f_rows(k, q, up, base + q)
        return remote(rows, rows, f_s.at[n], f_r.at[n], device(y + (1 if up else -1), h, z, l, c))

    def f_wait(k, q, up):
        n = (2 * k + q) * 2 + up
        rows = f_rows(k, q, up, 2 - base + q)
        remote(rows, rows, f_s.at[n], f_r.at[n], device(y + (1 if up else -1), h, z, l, c)).wait_recv()

    def e_copy(k, i, up, quarter):
        n = (2 * k + i) * 2 + up
        rows = slots.at[quarter, pl.ds((4 + k) * CAP, CAP), pl.ds(i * Q, Q)]
        return remote(rows, rows, e_s.at[n], e_r.at[n], device(y + (1 if up else -1), h, z, l, c))

    def v_copy(k, i, up, quarter):
        n = (2 * k + i) * 2 + up
        rows = slots.at[quarter, pl.ds((4 + k) * CAP + 32 * up, 32), pl.ds(i * Q, Q)]
        return remote(rows, rows, v_s.at[n], v_r.at[n], device(y + (1 if up else -1), h, z, l, c))

    everyone = (0,) + order

    def forward(q, which):
        for k in which:
            d_copy(0, k, 0, q).wait_recv()
            for up in range(2):
                f_copy(k, q, up).start()

    def spread(i, which):
        for k in which:
            d_copy(1, k, 0, i).wait_recv()
            for up in range(2):
                e_copy(k, i, up, y).start()

    def pass_on(i):
        for k in everyone:
            for up in range(2):
                quarter = (y + (3 if up else 1)) % 4
                e_copy(k, i, up, quarter).wait_recv()
                v_copy(k, i, up, quarter).start()

    def send_out(w, q, which):
        for k in which:
            each_peer(k, lambda cc, k=k: d_copy(w, k, cc, q).start())

    mine_rows = pl.ds(pl.multiple_of(c * CAP, CAP), CAP)

    def other_block(i):
        raw_copy(i).wait_recv()
        lanes = slice(i * Q, (i + 1) * Q)
        stage_oth[i] = dot(p_oth[...], raw[:, lanes]).astype(BF16)
        send_out(1, i, order + (0,))
        slots[y, 4 * CAP : 5 * CAP, lanes] = stage_oth[i, mine_rows]
        for up in range(2):
            e_copy(0, i, up, y).start()

    @pl.when(active)
    def _():
        raw_copy(0).start()
        each_meta(lambda copy: copy.start())
        for copy in own_copies:
            copy.wait()
        for q in range(2):
            stage[q] = dot(p_own[0:ROWS, :], xo[q]).astype(BF16)
            if q == 0:
                send_out(0, 0, order)
            send_out(0, q, (0,))
            slots[base + q, 0:CAP] = stage[q, mine_rows]
            for up in range(2):
                f_copy(0, q, up).start()
        raw_copy(0).wait_send()
        raw_copy(1).start()
        meta_copy(1, 0, 0).wait_recv()
        theirs = mb[4]
        first, second = named_by(theirs[0:1], theirs[1:2], expert_column(8))
        where = targets(first + second)
        for r in range(8):
            p_oth[r * CAP : (r + 1) * CAP] = one_hot(where[r : r + 1]).astype(BF16)
        other_block(0)
        forward(0, order)
        other_block(1)
        raw_copy(1).wait_send()
        for n in range(3):
            w_copy(n).start()

    @pl.when(idle)
    def _():
        for q in range(2):
            forward(q, (0,))
        spread(0, (0,))
        forward(0, order)
        for n in range(3):
            w_copy(n).start()
        spread(1, (0,))

    spread(0, order)

    @pl.when(active)
    def _():
        send_out(0, 1, order)

    spread(1, order)
    pass_on(0)
    forward(1, order)
    pass_on(1)

    @pl.when(idle)
    def _():
        meta_copy(0, 0, 0).wait_recv()
        meta_copy(1, 0, 0).wait_recv()

    for s in (1, 2, 3, 5, 6, 7):
        meta_copy(s // 4, s % 4, 0).wait_recv()
    mine = jnp.full((1, 1), ex, jnp.int32).astype(F32)
    firsts, seconds = named_by(mb[:, 0, :], mb[:, 1, :], mine)
    where = targets(firsts + seconds)
    weight = firsts * mb[:, 2, :] + seconds * mb[:, 3, :]
    for s in range(8):
        chosen = one_hot(where[s : s + 1]) * weight[s : s + 1]
        column = jnp.sum(chosen, axis=1, keepdims=True)
        pcol[s * CAP : (s + 1) * CAP] = jnp.broadcast_to(column, (CAP, 128))

    for copy in local:
        copy.wait()

    def inward_gu(j, w):
        rows = slice(w * HALF, (w + 1) * HALF)
        acc = jnp.zeros((HALF, 256), F32)
        for q in range(4):
            acc += dot_nt(slots[q, rows, 0:Q], wgu[j, :, q * Q : (q + 1) * Q])
        pre[j, rows] = acc

    def inward_d(j, w):
        rows = slice(w * HALF, (w + 1) * HALF)
        acc = jnp.zeros((HALF, 128), F32)
        for q in range(4):
            acc += dot_nt(slots[q, rows, Q : 2 * Q], wdn[j, :, q * Q : (q + 1) * Q])
        bk[j, rows] = acc

    def hidden_of(j, rows):
        gate = pre[j, rows, 0:128]
        up = pre[j, rows, 128:256]
        sig = jax.nn.sigmoid(gate)
        act = gate * sig
        return gate, up, sig, act, act * up

    def hidden_grads(j, rows):
        gate, up, sig, act, hidden = hidden_of(j, rows)
        backed = bk[j, rows]
        back = backed * pcol[rows]
        g_gate = back * up * sig * (1.0 + gate * (1.0 - sig))
        g_up = back * act
        ga[j, rows, 0:128] = g_gate.astype(BF16)
        ga[j, rows, 128:256] = g_up.astype(BF16)
        ga_t[j, 0:128, rows] = g_gate.T.astype(BF16)
        ga_t[j, 128:256, rows] = g_up.T.astype(BF16)
        return hidden, hidden * backed

    chunks = [slice(n * 128, n * 128 + 128) for n in range(4)]

    for w in range(2):
        for k in everyone:
            for i in range(2):
                for up in range(2):
                    if w == 0:
                        f_wait(k, i, up)
                    else:
                        v_copy(k, i, up, (y + 2) % 4).wait_recv()
        rows = slice(w * HALF, (w + 1) * HALF)
        for q in range(4):
            scaled[q, rows] = (slots[q, rows, Q : 2 * Q].astype(F32) * pcol[rows, 0:1]).astype(BF16)
        inward_gu(0, w)
        inward_d(0, w)
        for part in chunks[2 * w : 2 * w + 2]:
            hidden, terms = hidden_grads(0, part)
            hl_t[0, :, part] = hidden.T.astype(BF16)
            psum[part] = terms
        for q in range(4):
            dacc[q, rows] = dot(ga[0, rows], wgu[0, :, q * Q : (q + 1) * Q])
    for q in range(4):
        lanes = slice(q * Q, (q + 1) * Q)
        part = dot(ga_t[0], slots[q, :, 0:Q])
        o_g[0, :, lanes] = part[0:FF]
        o_u[0, :, lanes] = part[128 : 128 + FF]
        o_d[0, :, lanes] = dot(hl_t[0], scaled[q])[0:FF]

    @pl.when(active)
    def _():
        p_back[...] = p_own[...].astype(F32).T.astype(BF16)

    def gd_copy():
        return remote(gd_send, gd_recv, gd_s.at[0], gd_r.at[0], device(y, 1 - h, z, l, c))

    def g_copy(q):
        return remote(gsend.at[q], grecv.at[q], g_s.at[q], g_r.at[q], device(y, 1 - h, z, l, c))

    for n in range(2):
        w_copy(n).wait_recv()
    for w in range(2):
        inward_gu(1, w)
    for part in chunks:
        hl_t[1, :, part] = hidden_of(1, part)[4].T.astype(BF16)
    for q in range(4):
        gd_send[:, q * Q : (q + 1) * Q] = dot(hl_t[1], scaled[q]).astype(BF16)[0:FF]
    w_copy(2).wait_recv()
    gd_copy().start()

    def to(step):
        return device(y + step, h, z, l, c)

    def part_of(step, side, n):
        return dsend.at[(y + step + 4) % 4, side, pl.ds(n * 128, 128)]

    def rows_of(ref, side, n):
        return ref.at[side, pl.ds(n * 128, 128)]

    def far_copy(n, side):
        i = 2 * n + side
        return remote(
            part_of(2, side, n), rows_of(far, side, n), far_s.at[i], far_r.at[i], to(-1 if side == 0 else 1)
        )

    def near_copy(n, side):
        i = 2 * n + side
        step = 1 if side == 0 else -1
        return remote(part_of(step, side, n), rows_of(near, side, n), near_s.at[i], near_r.at[i], to(step))

    def chain_copy(n, side):
        i = 2 * n + side
        return remote(
            rows_of(csend, side, n),
            rows_of(chain, side, n),
            ch_s.at[i],
            ch_r.at[i],
            to(-1 if side == 0 else 1),
        )

    def pb_copy(s):
        w, k = s // 4, s % 4
        r = w * 8 + k * 2 + c
        return remote(pb.at[s], po.at[r], pb_s.at[s], pb_r.at[r], device(y, h, z - k, other(w), h))

    def each_owner(s, f):
        if s == 0:
            pl.when(idle)(f)
        else:
            f()

    def relay(n):
        for side in range(2):
            far_copy(n, side).wait_recv()
            step = -1 if side == 0 else 1
            rows = slice(n * 128, n * 128 + 128)
            total = far[side, rows].astype(F32) + dsend[(y + step + 4) % 4, side, rows].astype(F32)
            csend[side, rows] = total.astype(BF16)
            chain_copy(n, side).start()

    for n, part in enumerate(chunks):
        if n % 2 == 0:
            inward_d(1, n // 2)
        terms = hidden_grads(1, part)[1] + psum[part]
        column = jnp.sum(terms, axis=1, keepdims=True)
        for i in range(2):
            s = n * 2 + i
            row = jnp.sum(eye * column[i * CAP : (i + 1) * CAP], axis=0, keepdims=True)
            pb[s] = jnp.broadcast_to(row, (8, 128))
        for q in range(4):
            both = dacc[q, part] + dot(ga[1, part], wgu[1, :, q * Q : (q + 1) * Q])
            low = both.astype(BF16)
            dsend[q, 0, part] = low[:, 0:256]
            dsend[q, 1, part] = low[:, 256:512]
        for side in range(2):
            far_copy(n, side).start()
        for side in range(2):
            near_copy(n, side).start()
        for i in range(2):
            each_owner(n * 2 + i, lambda s=n * 2 + i: pb_copy(s).start())
        if n >= 2:
            relay(n - 2)

    def other_grads(q):
        part = dot(ga_t[1], slots[q, :, 0:Q]).astype(BF16)
        gsend[q, 0] = part[0:FF]
        gsend[q, 1] = part[128 : 128 + FF]
        g_copy(q).start()

    other_grads(0)
    relay(2)
    other_grads(1)
    relay(3)

    def rb_copy(s):
        w, k = s // 4, s % 4
        r = w * 8 + k * 2 + c
        return remote(
            dback.at[:, pl.ds(s * CAP, CAP)],
            down.at[:, pl.ds(pl.multiple_of(r * CAP, CAP), CAP)],
            rb_s.at[s],
            rb_r.at[r],
            device(y, h, z - k, other(w), h),
        )

    for n, part in enumerate(chunks):
        for side in range(2):
            near_copy(n, side).wait_recv()
            chain_copy(n, side).wait_recv()
            total = dsend[y, side, part].astype(F32) + near[side, part].astype(F32)
            dback[side, part] = (total + chain[side, part].astype(F32)).astype(BF16)
        for i in range(2):
            each_owner(n * 2 + i, lambda s=n * 2 + i: rb_copy(s).start())

    for q in (2, 3):
        other_grads(q)

    def add_down():
        gd_copy().wait_recv()
        o_d[0] = o_d[0] + gd_recv[...].astype(F32)

    def add_gate_up(q):
        g_copy(q).wait_recv()
        lanes = slice(q * Q, (q + 1) * Q)
        for n, out in enumerate((o_g, o_u)):
            out[0, :, lanes] = out[0, :, lanes] + grecv[q, n].astype(F32)

    def pf_copy(n):
        step, hh = n % 4, n // 4
        return remote(
            pf.at[0],
            pf.at[(4 - step) % 4],
            pf_s.at[n],
            pf_r.at[(4 - step) % 4],
            device(y + step, h if hh == 0 else 1 - h, z, l, c),
        )

    def t_copy():
        return remote(tsend, trecv, t_s.at[0], t_r.at[0], device(y, 1 - h, z, l, c))

    def owner_recv(w, copy):
        for k in range(4):
            each_peer(k if w == 0 else 4, lambda cc, k=k: copy(w * 8 + k * 2 + cc).wait_recv())

    @pl.when(active)
    def _():
        po[c] = pb[0]
        for w in range(2):
            owner_recv(
                w, lambda r: remote(pb.at[0], po.at[r], pb_s.at[0], pb_r.at[r], device(y, 1 - h, z, l, c))
            )
        first, second = named_by(meta[0:1], meta[1:2], expert_column(16))
        sums = [jnp.zeros((1, TOK), F32), jnp.zeros((1, TOK), F32)]
        for r in range(16):
            column = jnp.sum(eye * po[r, 0:1, :], axis=1, keepdims=True)
            row = jnp.sum(p_own[r * CAP : (r + 1) * CAP].astype(F32) * column, axis=0, keepdims=True)
            sums[0] += row * first[r : r + 1]
            sums[1] += row * second[r : r + 1]
        pf[0] = jnp.concatenate(sums + [jnp.zeros((6, TOK), F32)], axis=0)
        for n in range(1, 8):
            pf_copy(n).start()
        add_down()
        add_gate_up(0)
        add_gate_up(1)
        down[:, pl.ds(pl.multiple_of(c * CAP, CAP), CAP)] = dback[:, 0:CAP]
        sent = jnp.zeros((TOK, 256), F32)
        kept = jnp.zeros((TOK, 256), F32)
        for w in range(2):
            owner_recv(
                w,
                lambda r: remote(
                    dback.at[:, pl.ds(0, CAP)],
                    down.at[:, pl.ds(r * CAP, CAP)],
                    rb_s.at[0],
                    rb_r.at[r],
                    device(y, 1 - h, z, l, c),
                ),
            )
            rows = slice(w * ROWS, (w + 1) * ROWS)
            sent += dot(p_back[:, rows], down[1 - h, rows])
            if w == 1:
                tsend[...] = sent.astype(BF16)
                t_copy().start()
            kept += dot(p_back[:, rows], down[h, rows])
        o_tok[...] = kept

    @pl.when(idle)
    def _():
        add_down()
        add_gate_up(0)
        add_gate_up(1)
        t_copy().wait_recv()
        o_tok[...] = trecv[...].astype(F32)
        pf_copy(4).wait_recv()

    for n in (1, 2, 3):
        remote(pf.at[0], pf.at[n], pf_s.at[n], pf_r.at[n], device(y + n, h, z, l, c)).wait_recv()
    o_prob[...] = (pf[0] + pf[1] + pf[2] + pf[3])[0:2]

    for q in (2, 3):
        add_gate_up(q)

    @pl.when(active)
    def _():
        each_meta(lambda copy: copy.wait_send())
        for w in range(2):
            for q in range(2):
                for k in range(4):
                    each_peer(k, lambda cc, w=w, k=k, q=q: d_copy(w, k, cc, q).wait_send())
        for n in range(1, 8):
            pf_copy(n).wait_send()
        t_copy().wait_send()

    for n in range(3):
        w_copy(n).wait_send()
    for k in range(4):
        for i in range(2):
            for up in range(2):
                f_copy(k, i, up).wait_send()
                e_copy(k, i, up, y).wait_send()
                v_copy(k, i, up, (y + 1) % 4).wait_send()
    for s in range(8):

        def sent_back(s=s):
            pb_copy(s).wait_send()
            rb_copy(s).wait_send()

        each_owner(s, sent_back)
    for n in range(4):
        for side in range(2):
            far_copy(n, side).wait_send()
            near_copy(n, side).wait_send()
            chain_copy(n, side).wait_send()
    gd_copy().wait_send()
    for q in range(4):
        g_copy(q).wait_send()


def copy_out(*refs):
    copies = [pltpu.make_async_copy(refs[n], refs[5 + n], refs[10].at[n]) for n in range(5)]
    for copy in copies:
        copy.start()
    for copy in copies:
        copy.wait()


def in_hbm(value):
    return pltpu.with_memory_space_constraint(value, pltpu.HBM)


def on_device(tokens, out_grad, expert_ids, gate_probs, w_gate, w_up, w_down):
    dma = pltpu.SemaphoreType.DMA
    hbm = pl.BlockSpec(memory_space=pltpu.HBM)
    vmem = pl.BlockSpec(memory_space=pltpu.VMEM)
    outs = pl.pallas_call(
        kernel,
        out_shape=(
            jax.ShapeDtypeStruct((TOK, 256), F32),
            jax.ShapeDtypeStruct((2, TOK), F32),
            jax.ShapeDtypeStruct((1, FF, D), F32),
            jax.ShapeDtypeStruct((1, FF, D), F32),
            jax.ShapeDtypeStruct((1, FF, D), F32),
        ),
        in_specs=[hbm, hbm, vmem, vmem, hbm, hbm, hbm],
        out_specs=(vmem,) * 5,
        scratch_shapes=[
            pltpu.VMEM((8, TOK), F32),
            pltpu.VMEM((8, 8, TOK), F32),
            pltpu.VMEM((2, TOK, 2 * Q), BF16),
            pltpu.VMEM((TOK, 2 * Q), BF16),
            pltpu.VMEM((2, ROWS, 2 * Q), BF16),
            pltpu.VMEM((2, ROWS, Q), BF16),
            pltpu.VMEM((4, ROWS, 2 * Q), BF16),
            pltpu.VMEM((2, 256, D), BF16),
            pltpu.VMEM((2, 128, D), BF16),
            pltpu.VMEM((TOK, TOK), BF16),
            pltpu.VMEM((16 * CAP, TOK), BF16),
            pltpu.VMEM((TOK, 16 * CAP), BF16),
            pltpu.VMEM((8 * CAP, TOK), BF16),
            pltpu.VMEM((ROWS, 128), F32),
            pltpu.VMEM((2, ROWS, 256), F32),
            pltpu.VMEM((2, ROWS, 128), F32),
            pltpu.VMEM((2, ROWS, 256), BF16),
            pltpu.VMEM((2, 256, ROWS), BF16),
            pltpu.VMEM((2, 128, ROWS), BF16),
            pltpu.VMEM((ROWS, 128), F32),
            pltpu.VMEM((4, ROWS, Q), BF16),
            pltpu.VMEM((4, ROWS, Q), F32),
            pltpu.VMEM((4, 2, ROWS, 256), BF16),
            pltpu.VMEM((2, ROWS, 256), BF16),
            pltpu.VMEM((2, ROWS, 256), BF16),
            pltpu.VMEM((2, ROWS, 256), BF16),
            pltpu.VMEM((2, ROWS, 256), BF16),
            pltpu.VMEM((2, ROWS, 256), BF16),
            pltpu.VMEM((2, 16 * CAP, 256), BF16),
            pltpu.VMEM((8, 8, 128), F32),
            pltpu.VMEM((16, 8, 128), F32),
            pltpu.VMEM((4, 8, TOK), F32),
            pltpu.VMEM((FF, D), BF16),
            pltpu.VMEM((FF, D), BF16),
            pltpu.VMEM((4, 2, FF, Q), BF16),
            pltpu.VMEM((4, 2, FF, Q), BF16),
            pltpu.VMEM((TOK, 256), BF16),
            pltpu.VMEM((TOK, 256), BF16),
            dma((7,)),
            dma((16,)),
            dma((8,)),
            dma((2,)),
            dma((2,)),
            dma((3,)),
            dma((3,)),
            dma((32,)),
            dma((16,)),
            dma((16,)),
            dma((16,)),
            dma((16,)),
            dma((16,)),
            dma((16,)),
            dma((16,)),
            dma((8,)),
            dma((8,)),
            dma((8,)),
            dma((8,)),
            dma((8,)),
            dma((8,)),
            dma((8,)),
            dma((16,)),
            dma((8,)),
            dma((16,)),
            dma((1,)),
            dma((1,)),
            dma((4,)),
            dma((4,)),
            dma((1,)),
            dma((1,)),
            dma((8,)),
            dma((4,)),
        ],
        compiler_params=pltpu.CompilerParams(
            collective_id=0, has_side_effects=True, vmem_limit_bytes=48 << 20
        ),
        name="expert_backward",
    )(
        in_hbm(tokens),
        in_hbm(out_grad),
        expert_ids.T,
        gate_probs.T,
        in_hbm(w_gate),
        in_hbm(w_up),
        in_hbm(w_down),
    )
    token_grad, prob, grad_gate, grad_up, grad_down = pl.pallas_call(
        copy_out,
        out_shape=tuple(jax.ShapeDtypeStruct(v.shape, v.dtype) for v in outs),
        in_specs=[pl.BlockSpec(memory_space=pl.ANY)] * 5,
        out_specs=(pl.BlockSpec(memory_space=pl.ANY),) * 5,
        scratch_shapes=[dma((5,))],
        compiler_params=pltpu.CompilerParams(vmem_limit_bytes=1 << 20),
        name="copy_out",
    )(*outs)
    return token_grad, prob.T, grad_gate, grad_up, grad_down


def solution(mesh):
    in_specs = (
        P("expert", None),
        P("expert", None),
        P("expert", None),
        P("expert", None),
        P("expert", "dp", None),
        P("expert", "dp", None),
        P("expert", "dp", None),
    )
    out_specs = (
        P("expert", "dp"),
        P("expert", None),
        P("expert", "dp", None),
        P("expert", "dp", None),
        P("expert", "dp", None),
    )
    return jax.shard_map(
        on_device, mesh=mesh, in_specs=in_specs, out_specs=out_specs, check_vma=False
    )
```

```python
import jax
import jax.numpy as jnp
from jax import lax
from jax.experimental import pallas as pl
from jax.experimental.pallas import tpu as pltpu
from jax.sharding import PartitionSpec as P

MESH = pl.DeviceIdType.MESH
F32 = jnp.float32
BF16 = jnp.bfloat16

D = 2048
FF = 96
TOK = 256
CAP = 64
Q = 512
ROWS = 8 * CAP
HALF = ROWS // 2


def dot(a, b):
    return jnp.dot(a, b, preferred_element_type=F32)


def dot_nt(a, b):
    return lax.dot_general(a, b, (((1,), (1,)), ((), ())), preferred_element_type=F32)


def dot_tn(a, b):
    return lax.dot_general(a, b, (((0,), (0,)), ((), ())), preferred_element_type=F32)


def kernel(
    tok,
    dy,
    ids,
    prob,
    wg,
    wu,
    wd,
    o_tok,
    o_prob,
    o_g,
    o_u,
    o_d,
    meta,
    mb,
    xo,
    raw,
    stage,
    stage_oth,
    slots,
    wgu,
    wdn,
    upper,
    p_own,
    p_back,
    p_oth_back,
    p_oth,
    pcol,
    pre,
    bk,
    ga,
    ga_t,
    hl_t,
    psum,
    scaled,
    dacc,
    dsend,
    far,
    near,
    csend,
    chain,
    dback,
    down,
    pb,
    po,
    pf,
    gd_send,
    gd_recv,
    gsend,
    grecv,
    tsend,
    trecv,
    l_sem,
    m_s,
    m_r,
    raw_s,
    raw_r,
    w_s,
    w_r,
    d_s,
    d_r,
    f_s,
    f_r,
    e_s,
    e_r,
    v_s,
    v_r,
    far_s,
    far_r,
    near_s,
    near_r,
    ch_s,
    ch_r,
    pb_s,
    pb_r,
    rb_s,
    rb_r,
    gd_s,
    gd_r,
    g_s,
    g_r,
    t_s,
    t_r,
    pf_s,
    pf_r,
):
    dp = lax.axis_index("dp")
    ex = lax.axis_index("expert")
    y, h = dp // 2, dp % 2
    z, l, c = ex // 4, (ex // 2) % 2, ex % 2
    active = c == h
    idle = jnp.logical_not(active)
    base = (y % 2) * 2

    def device(yy, hh, zz, ll, cc):
        return (((yy + 4) % 4) * 2 + hh, ((zz + 4) % 4) * 4 + ll * 2 + cc)

    def remote(src, dst, send, recv, target):
        return pltpu.make_async_remote_copy(
            src_ref=src,
            dst_ref=dst,
            send_sem=send,
            recv_sem=recv,
            device_id=target,
            device_id_type=MESH,
        )

    def other(w):
        return l if w == 0 else 1 - l

    diagonal = device(y, 1 - h, z, 1 - l, c)

    barrier = pltpu.get_barrier_semaphore()
    for n in range(1, 16):
        pl.semaphore_signal(barrier, inc=1, device_id=(dp, (ex + n) % 16), device_id_type=MESH)
    for n in range(1, 8):
        pl.semaphore_signal(barrier, inc=1, device_id=((dp + n) % 8, ex), device_id_type=MESH)
    pl.semaphore_signal(barrier, inc=1, device_id=diagonal, device_id_type=MESH)

    local = [
        pltpu.make_async_copy(wg.at[0], wgu.at[0, pl.ds(0, FF)], l_sem.at[0]),
        pltpu.make_async_copy(wu.at[0], wgu.at[0, pl.ds(128, FF)], l_sem.at[1]),
        pltpu.make_async_copy(wd.at[0], wdn.at[0, pl.ds(0, FF)], l_sem.at[2]),
    ]

    def own_quarter(q):
        return (base + q) % 4

    def quarter_of(ref, q):
        return ref.at[:, pl.ds(pl.multiple_of(own_quarter(q) * Q, Q), Q)]

    own_copies = [
        pltpu.make_async_copy(quarter_of(ref, q), xo.at[q, :, pl.ds(i * Q, Q)], l_sem.at[3 + 2 * q + i])
        for q in (1, 0, 2)
        for i, ref in enumerate((tok, dy))
    ]

    @pl.when(active)
    def _():
        for copy in own_copies:
            copy.start()

    for copy in local:
        copy.start()
    meta[...] = jnp.concatenate(
        [ids[...].astype(F32), prob[...].astype(F32), jnp.zeros((4, TOK), F32)], axis=0
    )
    zeros = jnp.zeros((128 - FF, D), BF16)
    for j in range(2):
        wgu[j, FF:128] = zeros
        wgu[j, 128 + FF : 256] = zeros
        wdn[j, FF:128] = zeros
    upper[...] = (
        lax.broadcasted_iota(jnp.int32, (TOK, TOK), 0) < lax.broadcasted_iota(jnp.int32, (TOK, TOK), 1)
    ).astype(F32).astype(BF16)
    slot_iota = lax.broadcasted_iota(jnp.int32, (CAP, TOK), 0).astype(F32)
    eye = (
        lax.broadcasted_iota(jnp.int32, (CAP, 128), 0) == lax.broadcasted_iota(jnp.int32, (CAP, 128), 1)
    ).astype(F32)

    def targets(named):
        before = dot(named.astype(BF16), upper[...])
        return jnp.where(named > 0, before, -1.0)

    def one_hot(target_row):
        return (slot_iota == target_row).astype(F32)

    def named_by(ids0, ids1, experts):
        return (ids0 == experts).astype(F32), (ids1 == experts).astype(F32)

    def expert_column(count):
        r = lax.broadcasted_iota(jnp.int32, (count, 1), 0)
        return (4 * ((z + (r // 2) % 4) % 4) + 2 * ((l + r // 8) % 2) + r % 2).astype(F32)

    @pl.when(active)
    def _():
        mb[0] = meta[...]
        first, second = named_by(meta[0:1], meta[1:2], expert_column(16))
        where = targets(first + second)
        for r in range(16):
            p_own[r * CAP : (r + 1) * CAP] = one_hot(where[r : r + 1]).astype(BF16)

    pl.semaphore_wait(barrier, 23)

    def raw_copy(i):
        return remote(
            (tok, dy)[i].at[:, pl.ds(pl.multiple_of(y * Q, Q), Q)],
            raw.at[:, pl.ds(i * Q, Q)],
            raw_s.at[i],
            raw_r.at[i],
            device(y, h, z, 1 - l, c),
        )

    def meta_copy(w, k, cc):
        n = (w * 4 + k) * 2
        return remote(
            meta, mb.at[w * 4 + k], m_s.at[n + cc], m_r.at[w * 4 + k], device(y, h, z + k, other(w), cc)
        )

    def w_copy(n):
        src = (wg, wu, wd)[n]
        dst = (wgu.at[1, pl.ds(0, FF)], wgu.at[1, pl.ds(128, FF)], wdn.at[1, pl.ds(0, FF)])[n]
        return remote(src.at[0], dst, w_s.at[n], w_r.at[n], device(y, 1 - h, z, l, c))

    def each_peer(k, f):
        for cc in range(2):
            if k == 0:
                pl.when(cc != c)(lambda cc=cc: f(cc))
            else:
                f(cc)

    def each_meta(f):
        for w in range(2):
            for k in range(4):
                each_peer(k if w == 0 else 4, lambda cc, w=w, k=k: f(meta_copy(w, k, cc)))

    order = (1, 3, 2)

    def d_copy(w, k, cc, q):
        n = w * 24 + (k * 2 + cc) * 3 + q
        m = w * 12 + k * 3 + q
        rows = pl.ds((k * 2 + cc) * CAP, CAP)
        into = pl.ds((w * 4 + k) * CAP, CAP)
        return remote(
            stage.at[q, rows] if w == 0 else stage_oth.at[q, rows],
            slots.at[own_quarter(q), into] if w == 0 else slots.at[y, into, pl.ds(q * Q, Q)],
            d_s.at[n],
            d_r.at[m],
            device(y, h, z + k, l, cc),
        )

    def f_copy(k, up, quarter):
        n = 2 * k + up
        rows = slots.at[quarter, pl.ds(k * CAP + 32 * up, 32)]
        return remote(rows, rows, f_s.at[n], f_r.at[n], device(y + (1 if up else -1), h, z, l, c))

    def e_copy(k, i, up, quarter):
        n = (2 * k + i) * 2 + up
        rows = slots.at[quarter, pl.ds((4 + k) * CAP, CAP), pl.ds(i * Q, Q)]
        return remote(rows, rows, e_s.at[n], e_r.at[n], device(y + (1 if up else -1), h, z, l, c))

    def v_copy(k, i, up, quarter):
        n = (2 * k + i) * 2 + up
        rows = slots.at[quarter, pl.ds((4 + k) * CAP + 32 * up, 32), pl.ds(i * Q, Q)]
        return remote(rows, rows, v_s.at[n], v_r.at[n], device(y + (1 if up else -1), h, z, l, c))

    everyone = (0,) + order

    def forward(which):
        for k in which:
            d_copy(0, k, 0, 1).wait_recv()
            for up in range(2):
                f_copy(k, up, base + 1).start()

    def spread(i, which):
        for k in which:
            d_copy(1, k, 0, i).wait_recv()
            for up in range(2):
                e_copy(k, i, up, y).start()

    def pass_on(i):
        for k in everyone:
            for up in range(2):
                quarter = (y + (3 if up else 1)) % 4
                e_copy(k, i, up, quarter).wait_recv()
                v_copy(k, i, up, quarter).start()

    def send_out(w, q, which):
        for k in which:
            each_peer(k, lambda cc, k=k: d_copy(w, k, cc, q).start())

    mine_rows = pl.ds(pl.multiple_of(c * CAP, CAP), CAP)

    def other_block(i):
        raw_copy(i).wait_recv()
        lanes = slice(i * Q, (i + 1) * Q)
        stage_oth[i] = dot(p_oth[...], raw[:, lanes]).astype(BF16)
        send_out(1, i, order + (0,))
        slots[y, 4 * CAP : 5 * CAP, lanes] = stage_oth[i, mine_rows]
        for up in range(2):
            e_copy(0, i, up, y).start()

    def own_block(q):
        stage[q] = dot(p_own[0:ROWS, :], xo[q]).astype(BF16)
        slots[own_quarter(q), 0:CAP] = stage[q, mine_rows]

    @pl.when(active)
    def _():
        raw_copy(0).start()
        each_meta(lambda copy: copy.start())
        for copy in own_copies:
            copy.wait()
        own_block(1)
        send_out(0, 1, order + (0,))
        for up in range(2):
            f_copy(0, up, base + 1).start()
        raw_copy(0).wait_send()
        raw_copy(1).start()
        own_block(0)
        own_block(2)
        meta_copy(1, 0, 0).wait_recv()
        theirs = mb[4]
        first, second = named_by(theirs[0:1], theirs[1:2], expert_column(8))
        where = targets(first + second)
        for r in range(8):
            p_oth[r * CAP : (r + 1) * CAP] = one_hot(where[r : r + 1]).astype(BF16)
        other_block(0)
        raw_copy(1).wait_send()
        for n in range(2):
            w_copy(n).start()
        forward(order)
        other_block(1)

    @pl.when(idle)
    def _():
        forward((0,))
        spread(0, (0,))
        for n in range(2):
            w_copy(n).start()
        forward(order)
        spread(1, (0,))

    spread(0, order)

    @pl.when(active)
    def _():
        for q in (0, 2):
            send_out(0, q, order + (0,))

    spread(1, order)
    w_copy(2).start()
    pass_on(0)

    @pl.when(idle)
    def _():
        meta_copy(0, 0, 0).wait_recv()
        meta_copy(1, 0, 0).wait_recv()

    for s in (1, 2, 3, 5, 6, 7):
        meta_copy(s // 4, s % 4, 0).wait_recv()
    mine = jnp.full((1, 1), ex, jnp.int32).astype(F32)
    firsts, seconds = named_by(mb[:, 0, :], mb[:, 1, :], mine)
    where = targets(firsts + seconds)
    weight = firsts * mb[:, 2, :] + seconds * mb[:, 3, :]
    for s in range(8):
        chosen = one_hot(where[s : s + 1]) * weight[s : s + 1]
        column = jnp.sum(chosen, axis=1, keepdims=True)
        pcol[s * CAP : (s + 1) * CAP] = jnp.broadcast_to(column, (CAP, 128))

    pass_on(1)

    for copy in local:
        copy.wait()

    def inward_gu(j, w):
        rows = slice(w * HALF, (w + 1) * HALF)
        acc = jnp.zeros((HALF, 256), F32)
        for q in range(4):
            acc += dot_nt(slots[q, rows, 0:Q], wgu[j, :, q * Q : (q + 1) * Q])
        pre[j, rows] = acc

    def inward_d(j, w):
        rows = slice(w * HALF, (w + 1) * HALF)
        acc = jnp.zeros((HALF, 128), F32)
        for q in range(4):
            acc += dot_nt(slots[q, rows, Q : 2 * Q], wdn[j, :, q * Q : (q + 1) * Q])
        bk[j, rows] = acc

    def hidden_of(j, rows):
        gate = pre[j, rows, 0:128]
        up = pre[j, rows, 128:256]
        sig = jax.nn.sigmoid(gate)
        act = gate * sig
        return gate, up, sig, act, act * up

    def hidden_grads(j, rows):
        gate, up, sig, act, hidden = hidden_of(j, rows)
        backed = bk[j, rows]
        back = backed * pcol[rows]
        g_gate = back * up * sig * (1.0 + gate * (1.0 - sig))
        g_up = back * act
        ga[j, rows, 0:128] = g_gate.astype(BF16)
        ga[j, rows, 128:256] = g_up.astype(BF16)
        ga_t[j, 0:128, rows] = g_gate.T.astype(BF16)
        ga_t[j, 128:256, rows] = g_up.T.astype(BF16)
        return hidden, hidden * backed

    chunks = [slice(n * 128, n * 128 + 128) for n in range(4)]

    for w in range(2):
        if w == 0:
            pl.when(idle)(lambda: [d_copy(0, 0, 0, q).wait_recv() for q in (0, 2)][0])
            for k in order:
                for q in (0, 2):
                    d_copy(0, k, 0, q).wait_recv()
            for k in everyone:
                for up in range(2):
                    f_copy(k, up, 3 - base).wait_recv()
        else:
            for k in everyone:
                for i in range(2):
                    for up in range(2):
                        v_copy(k, i, up, (y + 2) % 4).wait_recv()
        rows = slice(w * HALF, (w + 1) * HALF)
        for q in range(4):
            scaled[q, rows] = (slots[q, rows, Q : 2 * Q].astype(F32) * pcol[rows, 0:1]).astype(BF16)
        inward_gu(0, w)
        inward_d(0, w)
        for part in chunks[2 * w : 2 * w + 2]:
            hidden, terms = hidden_grads(0, part)
            hl_t[0, :, part] = hidden.T.astype(BF16)
            psum[part] = terms
        for q in range(4):
            dacc[q, rows] = dot(ga[0, rows], wgu[0, :, q * Q : (q + 1) * Q])
        if w == 0:
            for n in range(2):
                w_copy(n).wait_recv()
        inward_gu(1, w)
        for part in chunks[2 * w : 2 * w + 2]:
            hl_t[1, :, part] = hidden_of(1, part)[4].T.astype(BF16)

    def gd_copy():
        return remote(gd_send, gd_recv, gd_s.at[0], gd_r.at[0], device(y, 1 - h, z, l, c))

    def g_copy(q):
        return remote(gsend.at[q], grecv.at[q], g_s.at[q], g_r.at[q], device(y, 1 - h, z, l, c))

    for q in range(4):
        gd_send[:, q * Q : (q + 1) * Q] = dot(hl_t[1], scaled[q]).astype(BF16)[0:FF]
    w_copy(2).wait_recv()
    gd_copy().start()

    def to(step):
        return device(y + step, h, z, l, c)

    def part_of(step, side, n):
        return dsend.at[(y + step + 4) % 4, side, pl.ds(n * 128, 128)]

    def rows_of(ref, side, n):
        return ref.at[side, pl.ds(n * 128, 128)]

    def far_copy(n, side):
        i = 2 * n + side
        return remote(
            part_of(2, side, n), rows_of(far, side, n), far_s.at[i], far_r.at[i], to(-1 if side == 0 else 1)
        )

    def near_copy(n, side):
        i = 2 * n + side
        step = 1 if side == 0 else -1
        return remote(part_of(step, side, n), rows_of(near, side, n), near_s.at[i], near_r.at[i], to(step))

    def chain_copy(n, side):
        i = 2 * n + side
        return remote(
            rows_of(csend, side, n),
            rows_of(chain, side, n),
            ch_s.at[i],
            ch_r.at[i],
            to(-1 if side == 0 else 1),
        )

    def pb_copy(s):
        w, k = s // 4, s % 4
        r = w * 8 + k * 2 + c
        return remote(pb.at[s], po.at[r], pb_s.at[s], pb_r.at[r], device(y, h, z - k, other(w), h))

    def each_owner(s, f):
        if s == 0:
            pl.when(idle)(f)
        else:
            f()

    def relay(n):
        for side in range(2):
            far_copy(n, side).wait_recv()
            step = -1 if side == 0 else 1
            rows = slice(n * 128, n * 128 + 128)
            total = far[side, rows].astype(F32) + dsend[(y + step + 4) % 4, side, rows].astype(F32)
            csend[side, rows] = total.astype(BF16)
            chain_copy(n, side).start()

    for n, part in enumerate(chunks):
        if n % 2 == 0:
            inward_d(1, n // 2)
        terms = hidden_grads(1, part)[1] + psum[part]
        column = jnp.sum(terms, axis=1, keepdims=True)
        for i in range(2):
            s = n * 2 + i
            row = jnp.sum(eye * column[i * CAP : (i + 1) * CAP], axis=0, keepdims=True)
            pb[s] = jnp.broadcast_to(row, (8, 128))
        for q in range(4):
            both = dacc[q, part] + dot(ga[1, part], wgu[1, :, q * Q : (q + 1) * Q])
            low = both.astype(BF16)
            dsend[q, 0, part] = low[:, 0:256]
            dsend[q, 1, part] = low[:, 256:512]
        for side in range(2):
            far_copy(n, side).start()
        for side in range(2):
            near_copy(n, side).start()
        for i in range(2):
            each_owner(n * 2 + i, lambda s=n * 2 + i: pb_copy(s).start())
        if n >= 2:
            relay(n - 2)

    def other_grads(q):
        part = dot(ga_t[1], slots[q, :, 0:Q]).astype(BF16)
        gsend[q, 0] = part[0:FF]
        gsend[q, 1] = part[128 : 128 + FF]
        g_copy(q).start()

    other_grads(0)
    relay(2)
    other_grads(1)
    relay(3)
    other_grads(2)

    for q in range(4):
        lanes = slice(q * Q, (q + 1) * Q)
        part = dot(ga_t[0], slots[q, :, 0:Q])
        o_g[0, :, lanes] = part[0:FF]
        o_u[0, :, lanes] = part[128 : 128 + FF]
        o_d[0, :, lanes] = dot(hl_t[0], scaled[q])[0:FF]

    @pl.when(active)
    def _():
        p_back[...] = p_own[0:ROWS].astype(F32).T.astype(BF16)
        p_oth_back[...] = p_oth[...].astype(F32).T.astype(BF16)

    def rb_copy(s):
        w, k = s // 4, s % 4
        r = w * 8 + k * 2 + c
        return remote(
            dback.at[:, pl.ds(s * CAP, CAP)],
            down.at[:, pl.ds(pl.multiple_of(r * CAP, CAP), CAP)],
            rb_s.at[s],
            rb_r.at[r],
            device(y, h, z - k, l, h),
        )

    def each_column(s, f):
        if s % 4 == 0:
            pl.when(idle)(f)
        else:
            f()

    for n, part in enumerate(chunks):
        for side in range(2):
            near_copy(n, side).wait_recv()
            chain_copy(n, side).wait_recv()
            total = dsend[y, side, part].astype(F32) + near[side, part].astype(F32)
            dback[side, part] = (total + chain[side, part].astype(F32)).astype(BF16)
        for i in range(2):
            each_column(n * 2 + i, lambda s=n * 2 + i: rb_copy(s).start())

    other_grads(3)

    def add_down():
        gd_copy().wait_recv()
        o_d[0] = o_d[0] + gd_recv[...].astype(F32)

    def add_gate_up(q):
        g_copy(q).wait_recv()
        lanes = slice(q * Q, (q + 1) * Q)
        for n, out in enumerate((o_g, o_u)):
            out[0, :, lanes] = out[0, :, lanes] + grecv[q, n].astype(F32)

    def pf_copy(n):
        step, hh = n % 4, n // 4
        return remote(
            pf.at[0],
            pf.at[(4 - step) % 4],
            pf_s.at[n],
            pf_r.at[(4 - step) % 4],
            device(y + step, h if hh == 0 else 1 - h, z, l, c),
        )

    def t_copy(n):
        target = (device(y, 1 - h, z, l, c), device(y, h, z, 1 - l, c), diagonal)[n]
        return remote(tsend.at[n], trecv.at[n], t_s.at[n], t_r.at[n], target)

    def recv_all(w, shared, copy):
        for k in range(4):
            each_peer(k if shared else 4, lambda cc, k=k: copy(w * 8 + k * 2 + cc).wait_recv())

    @pl.when(active)
    def _():
        po[c] = pb[0]
        for w in range(2):
            recv_all(
                w, w == 0, lambda r: remote(pb.at[0], po.at[r], pb_s.at[0], pb_r.at[r], device(y, 1 - h, z, l, c))
            )
        first, second = named_by(meta[0:1], meta[1:2], expert_column(16))
        sums = [jnp.zeros((1, TOK), F32), jnp.zeros((1, TOK), F32)]
        for r in range(16):
            column = jnp.sum(eye * po[r, 0:1, :], axis=1, keepdims=True)
            row = jnp.sum(p_own[r * CAP : (r + 1) * CAP].astype(F32) * column, axis=0, keepdims=True)
            sums[0] += row * first[r : r + 1]
            sums[1] += row * second[r : r + 1]
        pf[0] = jnp.concatenate(sums + [jnp.zeros((6, TOK), F32)], axis=0)
        for n in range(1, 8):
            pf_copy(n).start()
        add_down()
        add_gate_up(0)
        add_gate_up(1)
        for w in range(2):
            into = pl.ds(pl.multiple_of((w * 8 + c) * CAP, CAP), CAP)
            down[:, into] = dback[:, w * 4 * CAP : w * 4 * CAP + CAP]
            recv_all(
                w,
                True,
                lambda r: remote(
                    dback.at[:, pl.ds(0, CAP)],
                    down.at[:, pl.ds(r * CAP, CAP)],
                    rb_s.at[0],
                    rb_r.at[r],
                    device(y, 1 - h, z, l, c),
                ),
            )
            if w == 0:
                tsend[0] = dot(p_back[...], down[1 - h, 0:ROWS]).astype(BF16)
                t_copy(0).start()
                o_tok[...] = dot(p_back[...], down[h, 0:ROWS])
            else:
                tsend[1] = dot(p_oth_back[...], down[h, ROWS : 2 * ROWS]).astype(BF16)
                t_copy(1).start()
                tsend[2] = dot(p_oth_back[...], down[1 - h, ROWS : 2 * ROWS]).astype(BF16)
                t_copy(2).start()
        t_copy(1).wait_recv()
        o_tok[...] = o_tok[...] + trecv[1].astype(F32)

    @pl.when(idle)
    def _():
        add_down()
        add_gate_up(0)
        add_gate_up(1)
        t_copy(0).wait_recv()
        t_copy(2).wait_recv()
        o_tok[...] = trecv[0].astype(F32) + trecv[2].astype(F32)
        pf_copy(4).wait_recv()

    for n in (1, 2, 3):
        remote(pf.at[0], pf.at[n], pf_s.at[n], pf_r.at[n], device(y + n, h, z, l, c)).wait_recv()
    o_prob[...] = (pf[0] + pf[1] + pf[2] + pf[3])[0:2]

    for q in (2, 3):
        add_gate_up(q)

    @pl.when(active)
    def _():
        each_meta(lambda copy: copy.wait_send())
        for w in range(2):
            for q in range(3 - w):
                for k in range(4):
                    each_peer(k, lambda cc, w=w, k=k, q=q: d_copy(w, k, cc, q).wait_send())
        for n in range(1, 8):
            pf_copy(n).wait_send()
        for n in range(3):
            t_copy(n).wait_send()

    for n in range(3):
        w_copy(n).wait_send()
    for k in range(4):
        for up in range(2):
            f_copy(k, up, base + 1).wait_send()
            for i in range(2):
                e_copy(k, i, up, y).wait_send()
                v_copy(k, i, up, (y + 1) % 4).wait_send()
    for s in range(8):

        each_owner(s, lambda s=s: pb_copy(s).wait_send())
        each_column(s, lambda s=s: rb_copy(s).wait_send())
    for n in range(4):
        for side in range(2):
            far_copy(n, side).wait_send()
            near_copy(n, side).wait_send()
            chain_copy(n, side).wait_send()
    gd_copy().wait_send()
    for q in range(4):
        g_copy(q).wait_send()


def copy_out(*refs):
    copies = [pltpu.make_async_copy(refs[n], refs[5 + n], refs[10].at[n]) for n in range(5)]
    for copy in copies:
        copy.start()
    for copy in copies:
        copy.wait()


def in_hbm(value):
    return pltpu.with_memory_space_constraint(value, pltpu.HBM)


def on_device(tokens, out_grad, expert_ids, gate_probs, w_gate, w_up, w_down):
    dma = pltpu.SemaphoreType.DMA
    hbm = pl.BlockSpec(memory_space=pltpu.HBM)
    vmem = pl.BlockSpec(memory_space=pltpu.VMEM)
    outs = pl.pallas_call(
        kernel,
        out_shape=(
            jax.ShapeDtypeStruct((TOK, 256), F32),
            jax.ShapeDtypeStruct((2, TOK), F32),
            jax.ShapeDtypeStruct((1, FF, D), F32),
            jax.ShapeDtypeStruct((1, FF, D), F32),
            jax.ShapeDtypeStruct((1, FF, D), F32),
        ),
        in_specs=[hbm, hbm, vmem, vmem, hbm, hbm, hbm],
        out_specs=(vmem,) * 5,
        scratch_shapes=[
            pltpu.VMEM((8, TOK), F32),
            pltpu.VMEM((8, 8, TOK), F32),
            pltpu.VMEM((3, TOK, 2 * Q), BF16),
            pltpu.VMEM((TOK, 2 * Q), BF16),
            pltpu.VMEM((3, ROWS, 2 * Q), BF16),
            pltpu.VMEM((2, ROWS, Q), BF16),
            pltpu.VMEM((4, ROWS, 2 * Q), BF16),
            pltpu.VMEM((2, 256, D), BF16),
            pltpu.VMEM((2, 128, D), BF16),
            pltpu.VMEM((TOK, TOK), BF16),
            pltpu.VMEM((16 * CAP, TOK), BF16),
            pltpu.VMEM((TOK, ROWS), BF16),
            pltpu.VMEM((TOK, ROWS), BF16),
            pltpu.VMEM((8 * CAP, TOK), BF16),
            pltpu.VMEM((ROWS, 128), F32),
            pltpu.VMEM((2, ROWS, 256), F32),
            pltpu.VMEM((2, ROWS, 128), F32),
            pltpu.VMEM((2, ROWS, 256), BF16),
            pltpu.VMEM((2, 256, ROWS), BF16),
            pltpu.VMEM((2, 128, ROWS), BF16),
            pltpu.VMEM((ROWS, 128), F32),
            pltpu.VMEM((4, ROWS, Q), BF16),
            pltpu.VMEM((4, ROWS, Q), F32),
            pltpu.VMEM((4, 2, ROWS, 256), BF16),
            pltpu.VMEM((2, ROWS, 256), BF16),
            pltpu.VMEM((2, ROWS, 256), BF16),
            pltpu.VMEM((2, ROWS, 256), BF16),
            pltpu.VMEM((2, ROWS, 256), BF16),
            pltpu.VMEM((2, ROWS, 256), BF16),
            pltpu.VMEM((2, 16 * CAP, 256), BF16),
            pltpu.VMEM((8, 8, 128), F32),
            pltpu.VMEM((16, 8, 128), F32),
            pltpu.VMEM((4, 8, TOK), F32),
            pltpu.VMEM((FF, D), BF16),
            pltpu.VMEM((FF, D), BF16),
            pltpu.VMEM((4, 2, FF, Q), BF16),
            pltpu.VMEM((4, 2, FF, Q), BF16),
            pltpu.VMEM((3, TOK, 256), BF16),
            pltpu.VMEM((3, TOK, 256), BF16),
            dma((9,)),
            dma((16,)),
            dma((8,)),
            dma((2,)),
            dma((2,)),
            dma((3,)),
            dma((3,)),
            dma((48,)),
            dma((24,)),
            dma((8,)),
            dma((8,)),
            dma((16,)),
            dma((16,)),
            dma((16,)),
            dma((16,)),
            dma((8,)),
            dma((8,)),
            dma((8,)),
            dma((8,)),
            dma((8,)),
            dma((8,)),
            dma((8,)),
            dma((16,)),
            dma((8,)),
            dma((16,)),
            dma((1,)),
            dma((1,)),
            dma((4,)),
            dma((4,)),
            dma((3,)),
            dma((3,)),
            dma((8,)),
            dma((4,)),
        ],
        compiler_params=pltpu.CompilerParams(
            collective_id=0, has_side_effects=True, vmem_limit_bytes=48 << 20
        ),
        name="expert_backward",
    )(
        in_hbm(tokens),
        in_hbm(out_grad),
        expert_ids.T,
        gate_probs.T,
        in_hbm(w_gate),
        in_hbm(w_up),
        in_hbm(w_down),
    )
    token_grad, prob, grad_gate, grad_up, grad_down = pl.pallas_call(
        copy_out,
        out_shape=tuple(jax.ShapeDtypeStruct(v.shape, v.dtype) for v in outs),
        in_specs=[pl.BlockSpec(memory_space=pl.ANY)] * 5,
        out_specs=(pl.BlockSpec(memory_space=pl.ANY),) * 5,
        scratch_shapes=[dma((5,))],
        compiler_params=pltpu.CompilerParams(vmem_limit_bytes=1 << 20),
        name="copy_out",
    )(*outs)
    return token_grad, prob.T, grad_gate, grad_up, grad_down


def solution(mesh):
    in_specs = (
        P("expert", None),
        P("expert", None),
        P("expert", None),
        P("expert", None),
        P("expert", "dp", None),
        P("expert", "dp", None),
        P("expert", "dp", None),
    )
    out_specs = (
        P("expert", "dp"),
        P("expert", None),
        P("expert", "dp", None),
        P("expert", "dp", None),
        P("expert", "dp", None),
    )
    return jax.shard_map(
        on_device, mesh=mesh, in_specs=in_specs, out_specs=out_specs, check_vma=False
    )
```

```python
import jax
import jax.numpy as jnp
from jax import lax
from jax.experimental import pallas as pl
from jax.experimental.pallas import tpu as pltpu
from jax.sharding import PartitionSpec as P

MESH = pl.DeviceIdType.MESH
F32 = jnp.float32
BF16 = jnp.bfloat16

D = 2048
FF = 96
TOK = 256
CAP = 64
Q = 512
ROWS = 8 * CAP
HALF = ROWS // 2


def dot(a, b):
    return jnp.dot(a, b, preferred_element_type=F32)


def dot_nt(a, b):
    return lax.dot_general(a, b, (((1,), (1,)), ((), ())), preferred_element_type=F32)


def dot_tn(a, b):
    return lax.dot_general(a, b, (((0,), (0,)), ((), ())), preferred_element_type=F32)


def kernel(
    tok,
    dy,
    ids,
    prob,
    wg,
    wu,
    wd,
    o_tok,
    o_prob,
    o_g,
    o_u,
    o_d,
    meta,
    mb,
    xo,
    raw,
    stage,
    stage_oth,
    slots,
    wgu,
    wdn,
    upper,
    p_own,
    p_back,
    p_oth_back,
    p_oth,
    pcol,
    pre,
    bk,
    ga,
    ga_t,
    hl_t,
    psum,
    scaled,
    dacc,
    dsend,
    far,
    near,
    csend,
    chain,
    dback,
    down,
    pb,
    po,
    pf,
    gd_send,
    gd_recv,
    gsend,
    grecv,
    tsend,
    trecv,
    l_sem,
    m_s,
    m_r,
    raw_s,
    raw_r,
    w_s,
    w_r,
    d_s,
    d_r,
    f_s,
    f_r,
    e_s,
    e_r,
    v_s,
    v_r,
    far_s,
    far_r,
    near_s,
    near_r,
    ch_s,
    ch_r,
    pb_s,
    pb_r,
    rb_s,
    rb_r,
    gd_s,
    gd_r,
    g_s,
    g_r,
    t_s,
    t_r,
    pf_s,
    pf_r,
):
    dp = lax.axis_index("dp")
    ex = lax.axis_index("expert")
    y, h = dp // 2, dp % 2
    z, l, c = ex // 4, (ex // 2) % 2, ex % 2
    active = c == h
    idle = jnp.logical_not(active)
    base = (y % 2) * 2

    def device(yy, hh, zz, ll, cc):
        return (((yy + 4) % 4) * 2 + hh, ((zz + 4) % 4) * 4 + ll * 2 + cc)

    def remote(src, dst, send, recv, target):
        return pltpu.make_async_remote_copy(
            src_ref=src,
            dst_ref=dst,
            send_sem=send,
            recv_sem=recv,
            device_id=target,
            device_id_type=MESH,
        )

    def other(w):
        return l if w == 0 else 1 - l

    diagonal = device(y, 1 - h, z, 1 - l, c)

    barrier = pltpu.get_barrier_semaphore()
    for n in range(1, 16):
        pl.semaphore_signal(barrier, inc=1, device_id=(dp, (ex + n) % 16), device_id_type=MESH)
    for n in range(1, 8):
        pl.semaphore_signal(barrier, inc=1, device_id=((dp + n) % 8, ex), device_id_type=MESH)
    pl.semaphore_signal(barrier, inc=1, device_id=diagonal, device_id_type=MESH)

    local = [
        pltpu.make_async_copy(wg.at[0], wgu.at[0, pl.ds(0, FF)], l_sem.at[0]),
        pltpu.make_async_copy(wu.at[0], wgu.at[0, pl.ds(128, FF)], l_sem.at[1]),
        pltpu.make_async_copy(wd.at[0], wdn.at[0, pl.ds(0, FF)], l_sem.at[2]),
    ]

    def own_quarter(q):
        return (base + q) % 4

    def quarter_of(ref, q):
        return ref.at[:, pl.ds(pl.multiple_of(own_quarter(q) * Q, Q), Q)]

    own_copies = [
        pltpu.make_async_copy(quarter_of(ref, q), xo.at[q, :, pl.ds(i * Q, Q)], l_sem.at[3 + 2 * q + i])
        for q in (1, 0, 2)
        for i, ref in enumerate((tok, dy))
    ]

    @pl.when(active)
    def _():
        for copy in own_copies:
            copy.start()

    for copy in local:
        copy.start()
    meta[...] = jnp.concatenate(
        [ids[...].astype(F32), prob[...].astype(F32), jnp.zeros((4, TOK), F32)], axis=0
    )
    zeros = jnp.zeros((128 - FF, D), BF16)
    for j in range(2):
        wgu[j, FF:128] = zeros
        wgu[j, 128 + FF : 256] = zeros
        wdn[j, FF:128] = zeros
    upper[...] = (
        lax.broadcasted_iota(jnp.int32, (TOK, TOK), 0) < lax.broadcasted_iota(jnp.int32, (TOK, TOK), 1)
    ).astype(F32).astype(BF16)
    slot_iota = lax.broadcasted_iota(jnp.int32, (CAP, TOK), 0).astype(F32)
    eye = (
        lax.broadcasted_iota(jnp.int32, (CAP, 128), 0) == lax.broadcasted_iota(jnp.int32, (CAP, 128), 1)
    ).astype(F32)

    def targets(named):
        before = dot(named.astype(BF16), upper[...])
        return jnp.where(named > 0, before, -1.0)

    def one_hot(target_row):
        return (slot_iota == target_row).astype(F32)

    def named_by(ids0, ids1, experts):
        return (ids0 == experts).astype(F32), (ids1 == experts).astype(F32)

    def expert_column(count):
        r = lax.broadcasted_iota(jnp.int32, (count, 1), 0)
        return (4 * ((z + (r // 2) % 4) % 4) + 2 * ((l + r // 8) % 2) + r % 2).astype(F32)

    @pl.when(active)
    def _():
        mb[0] = meta[...]
        first, second = named_by(meta[0:1], meta[1:2], expert_column(16))
        where = targets(first + second)
        for r in range(16):
            p_own[r * CAP : (r + 1) * CAP] = one_hot(where[r : r + 1]).astype(BF16)

    pl.semaphore_wait(barrier, 23)

    def raw_copy(i):
        return remote(
            (tok, dy)[i].at[:, pl.ds(pl.multiple_of(y * Q, Q), Q)],
            raw.at[:, pl.ds(i * Q, Q)],
            raw_s.at[i],
            raw_r.at[i],
            device(y, h, z, 1 - l, c) if i == 0 else diagonal,
        )

    def meta_copy(w, k, cc):
        n = (w * 4 + k) * 2
        return remote(
            meta, mb.at[w * 4 + k], m_s.at[n + cc], m_r.at[w * 4 + k], device(y, h, z + k, other(w), cc)
        )

    def w_copy(n):
        src = (wg, wu, wd)[n]
        dst = (wgu.at[1, pl.ds(0, FF)], wgu.at[1, pl.ds(128, FF)], wdn.at[1, pl.ds(0, FF)])[n]
        return remote(src.at[0], dst, w_s.at[n], w_r.at[n], device(y, 1 - h, z, l, c))

    def each_peer(k, f):
        for cc in range(2):
            if k == 0:
                pl.when(cc != c)(lambda cc=cc: f(cc))
            else:
                f(cc)

    def each_meta(f):
        for w in range(2):
            for k in range(4):
                each_peer(k if w == 0 else 4, lambda cc, w=w, k=k: f(meta_copy(w, k, cc)))

    order = (1, 3, 2)

    def d_copy(w, k, cc, q):
        n = w * 24 + (k * 2 + cc) * 3 + q
        m = w * 12 + k * 3 + q
        rows = pl.ds((k * 2 + cc) * CAP, CAP)
        into = pl.ds((w * 4 + k) * CAP, CAP)
        return remote(
            stage.at[q, rows] if w == 0 else stage_oth.at[q, rows],
            slots.at[own_quarter(q), into] if w == 0 else slots.at[y, into, pl.ds(q * Q, Q)],
            d_s.at[n],
            d_r.at[m],
            device(y, h, z + k, l, cc),
        )

    def f_copy(k, up, quarter):
        n = 2 * k + up
        rows = slots.at[quarter, pl.ds(k * CAP + 32 * up, 32)]
        return remote(rows, rows, f_s.at[n], f_r.at[n], device(y + (1 if up else -1), h, z, l, c))

    def e_copy(k, i, up, quarter):
        n = (2 * k + i) * 2 + up
        rows = slots.at[quarter, pl.ds((4 + k) * CAP, CAP), pl.ds(i * Q, Q)]
        return remote(rows, rows, e_s.at[n], e_r.at[n], device(y + (1 if up else -1), h, z, l, c))

    def v_copy(k, i, up, quarter):
        n = (2 * k + i) * 2 + up
        rows = slots.at[quarter, pl.ds((4 + k) * CAP + 32 * up, 32), pl.ds(i * Q, Q)]
        return remote(rows, rows, v_s.at[n], v_r.at[n], device(y + (1 if up else -1), h, z, l, c))

    everyone = (0,) + order

    def forward(which):
        for k in which:
            d_copy(0, k, 0, 1).wait_recv()
            for up in range(2):
                f_copy(k, up, base + 1).start()

    def spread(i, which):
        for k in which:
            d_copy(1, k, 0, i).wait_recv()
            for up in range(2):
                e_copy(k, i, up, y).start()

    def pass_on(i):
        for k in everyone:
            for up in range(2):
                quarter = (y + (3 if up else 1)) % 4
                e_copy(k, i, up, quarter).wait_recv()
                v_copy(k, i, up, quarter).start()

    def send_out(w, q, which):
        for k in which:
            each_peer(k, lambda cc, k=k: d_copy(w, k, cc, q).start())

    mine_rows = pl.ds(pl.multiple_of(c * CAP, CAP), CAP)

    def other_block(i):
        raw_copy(i).wait_recv()
        lanes = slice(i * Q, (i + 1) * Q)
        stage_oth[i] = dot(p_oth[...], raw[:, lanes]).astype(BF16)
        send_out(1, i, order + (0,))
        slots[y, 4 * CAP : 5 * CAP, lanes] = stage_oth[i, mine_rows]
        for up in range(2):
            e_copy(0, i, up, y).start()

    def own_block(q):
        stage[q] = dot(p_own[0:ROWS, :], xo[q]).astype(BF16)
        slots[own_quarter(q), 0:CAP] = stage[q, mine_rows]

    @pl.when(active)
    def _():
        raw_copy(0).start()
        each_meta(lambda copy: copy.start())
        for copy in own_copies:
            copy.wait()
        own_block(1)
        send_out(0, 1, order + (0,))
        for up in range(2):
            f_copy(0, up, base + 1).start()
        own_block(0)
        own_block(2)
        meta_copy(1, 0, 0).wait_recv()
        theirs = mb[4]
        first, second = named_by(theirs[0:1], theirs[1:2], expert_column(8))
        where = targets(first + second)
        for r in range(8):
            p_oth[r * CAP : (r + 1) * CAP] = one_hot(where[r : r + 1]).astype(BF16)
        other_block(0)
        raw_copy(0).wait_send()
        for n in range(2):
            w_copy(n).start()
        forward(order)
        other_block(1)

    @pl.when(idle)
    def _():
        raw_copy(1).start()
        forward((0,))
        raw_copy(1).wait_send()
        for n in range(2):
            w_copy(n).start()
        spread(0, (0,))
        forward(order)
        spread(1, (0,))

    spread(0, order)

    @pl.when(active)
    def _():
        for q in (0, 2):
            send_out(0, q, order + (0,))

    spread(1, order)
    w_copy(2).start()
    pass_on(0)

    @pl.when(idle)
    def _():
        meta_copy(0, 0, 0).wait_recv()
        meta_copy(1, 0, 0).wait_recv()

    for s in (1, 2, 3, 5, 6, 7):
        meta_copy(s // 4, s % 4, 0).wait_recv()
    mine = jnp.full((1, 1), ex, jnp.int32).astype(F32)
    firsts, seconds = named_by(mb[:, 0, :], mb[:, 1, :], mine)
    where = targets(firsts + seconds)
    weight = firsts * mb[:, 2, :] + seconds * mb[:, 3, :]
    for s in range(8):
        chosen = one_hot(where[s : s + 1]) * weight[s : s + 1]
        column = jnp.sum(chosen, axis=1, keepdims=True)
        pcol[s * CAP : (s + 1) * CAP] = jnp.broadcast_to(column, (CAP, 128))

    pass_on(1)

    for copy in local:
        copy.wait()

    def inward_gu(j, w):
        rows = slice(w * HALF, (w + 1) * HALF)
        acc = jnp.zeros((HALF, 256), F32)
        for q in range(4):
            acc += dot_nt(slots[q, rows, 0:Q], wgu[j, :, q * Q : (q + 1) * Q])
        pre[j, rows] = acc

    def inward_d(j, w):
        rows = slice(w * HALF, (w + 1) * HALF)
        acc = jnp.zeros((HALF, 128), F32)
        for q in range(4):
            acc += dot_nt(slots[q, rows, Q : 2 * Q], wdn[j, :, q * Q : (q + 1) * Q])
        bk[j, rows] = acc

    def hidden_of(j, rows):
        gate = pre[j, rows, 0:128]
        up = pre[j, rows, 128:256]
        sig = jax.nn.sigmoid(gate)
        act = gate * sig
        return gate, up, sig, act, act * up

    def hidden_grads(j, rows):
        gate, up, sig, act, hidden = hidden_of(j, rows)
        backed = bk[j, rows]
        back = backed * pcol[rows]
        g_gate = back * up * sig * (1.0 + gate * (1.0 - sig))
        g_up = back * act
        ga[j, rows, 0:128] = g_gate.astype(BF16)
        ga[j, rows, 128:256] = g_up.astype(BF16)
        ga_t[j, 0:128, rows] = g_gate.T.astype(BF16)
        ga_t[j, 128:256, rows] = g_up.T.astype(BF16)
        return hidden, hidden * backed

    chunks = [slice(n * 128, n * 128 + 128) for n in range(4)]

    for w in range(2):
        if w == 0:
            pl.when(idle)(lambda: [d_copy(0, 0, 0, q).wait_recv() for q in (0, 2)][0])
            for k in order:
                for q in (0, 2):
                    d_copy(0, k, 0, q).wait_recv()
            for k in everyone:
                for up in range(2):
                    f_copy(k, up, 3 - base).wait_recv()
        else:
            for k in everyone:
                for i in range(2):
                    for up in range(2):
                        v_copy(k, i, up, (y + 2) % 4).wait_recv()
        rows = slice(w * HALF, (w + 1) * HALF)
        for q in range(4):
            scaled[q, rows] = (slots[q, rows, Q : 2 * Q].astype(F32) * pcol[rows, 0:1]).astype(BF16)
        inward_gu(0, w)
        inward_d(0, w)
        for part in chunks[2 * w : 2 * w + 2]:
            hidden, terms = hidden_grads(0, part)
            hl_t[0, :, part] = hidden.T.astype(BF16)
            psum[part] = terms
        for q in range(4):
            dacc[q, rows] = dot(ga[0, rows], wgu[0, :, q * Q : (q + 1) * Q])
        if w == 0:
            for n in range(2):
                w_copy(n).wait_recv()
        inward_gu(1, w)
        for part in chunks[2 * w : 2 * w + 2]:
            hl_t[1, :, part] = hidden_of(1, part)[4].T.astype(BF16)

    def gd_copy():
        return remote(gd_send, gd_recv, gd_s.at[0], gd_r.at[0], device(y, 1 - h, z, l, c))

    def g_copy(q):
        return remote(gsend.at[q], grecv.at[q], g_s.at[q], g_r.at[q], device(y, 1 - h, z, l, c))

    for q in range(4):
        gd_send[:, q * Q : (q + 1) * Q] = dot(hl_t[1], scaled[q]).astype(BF16)[0:FF]
    w_copy(2).wait_recv()
    gd_copy().start()

    def to(step):
        return device(y + step, h, z, l, c)

    def part_of(step, side, n):
        return dsend.at[(y + step + 4) % 4, side, pl.ds(n * 128, 128)]

    def rows_of(ref, side, n):
        return ref.at[side, pl.ds(n * 128, 128)]

    def far_copy(n, side):
        i = 2 * n + side
        return remote(
            part_of(2, side, n), rows_of(far, side, n), far_s.at[i], far_r.at[i], to(-1 if side == 0 else 1)
        )

    def near_copy(n, side):
        i = 2 * n + side
        step = 1 if side == 0 else -1
        return remote(part_of(step, side, n), rows_of(near, side, n), near_s.at[i], near_r.at[i], to(step))

    def chain_copy(n, side):
        i = 2 * n + side
        return remote(
            rows_of(csend, side, n),
            rows_of(chain, side, n),
            ch_s.at[i],
            ch_r.at[i],
            to(-1 if side == 0 else 1),
        )

    def pb_copy(s):
        w, k = s // 4, s % 4
        r = w * 8 + k * 2 + c
        return remote(pb.at[s], po.at[r], pb_s.at[s], pb_r.at[r], device(y, h, z - k, other(w), h))

    def each_owner(s, f):
        if s == 0:
            pl.when(idle)(f)
        else:
            f()

    def relay(n):
        for side in range(2):
            far_copy(n, side).wait_recv()
            step = -1 if side == 0 else 1
            rows = slice(n * 128, n * 128 + 128)
            total = far[side, rows].astype(F32) + dsend[(y + step + 4) % 4, side, rows].astype(F32)
            csend[side, rows] = total.astype(BF16)
            chain_copy(n, side).start()

    def chunk(n):
        part = chunks[n]
        if n % 2 == 0:
            inward_d(1, n // 2)
        terms = hidden_grads(1, part)[1] + psum[part]
        column = jnp.sum(terms, axis=1, keepdims=True)
        for i in range(2):
            s = n * 2 + i
            row = jnp.sum(eye * column[i * CAP : (i + 1) * CAP], axis=0, keepdims=True)
            pb[s] = jnp.broadcast_to(row, (8, 128))
        for q in range(4):
            both = dacc[q, part] + dot(ga[1, part], wgu[1, :, q * Q : (q + 1) * Q])
            low = both.astype(BF16)
            dsend[q, 0, part] = low[:, 0:256]
            dsend[q, 1, part] = low[:, 256:512]
        for side in range(2):
            far_copy(n, side).start()
        for i in range(2):
            each_owner(n * 2 + i, lambda s=n * 2 + i: pb_copy(s).start())

    def near_sums(n):
        for side in range(2):
            near_copy(n, side).start()

    def other_grads(q):
        part = dot(ga_t[1], slots[q, :, 0:Q]).astype(BF16)
        gsend[q, 0] = part[0:FF]
        gsend[q, 1] = part[128 : 128 + FF]
        g_copy(q).start()

    def own_grads():
        for q in range(4):
            lanes = slice(q * Q, (q + 1) * Q)
            part = dot(ga_t[0], slots[q, :, 0:Q])
            o_g[0, :, lanes] = part[0:FF]
            o_u[0, :, lanes] = part[128 : 128 + FF]
            o_d[0, :, lanes] = dot(hl_t[0], scaled[q])[0:FF]

        @pl.when(active)
        def _():
            p_back[...] = p_own[0:ROWS].astype(F32).T.astype(BF16)
            p_oth_back[...] = p_oth[...].astype(F32).T.astype(BF16)

    def rb_copy(s):
        w, k = s // 4, s % 4
        r = w * 8 + k * 2 + c
        return remote(
            dback.at[:, pl.ds(s * CAP, CAP)],
            down.at[:, pl.ds(pl.multiple_of(r * CAP, CAP), CAP)],
            rb_s.at[s],
            rb_r.at[r],
            device(y, h, z - k, l, h),
        )

    def each_column(s, f):
        if s % 4 == 0:
            pl.when(idle)(f)
        else:
            f()

    def back(n):
        part = chunks[n]
        for side in range(2):
            near_copy(n, side).wait_recv()
            chain_copy(n, side).wait_recv()
            total = dsend[y, side, part].astype(F32) + near[side, part].astype(F32)
            dback[side, part] = (total + chain[side, part].astype(F32)).astype(BF16)
        for i in range(2):
            each_column(n * 2 + i, lambda s=n * 2 + i: rb_copy(s).start())

    def add_down():
        gd_copy().wait_recv()
        o_d[0] = o_d[0] + gd_recv[...].astype(F32)

    def add_gate_up(q):
        g_copy(q).wait_recv()
        lanes = slice(q * Q, (q + 1) * Q)
        for n, out in enumerate((o_g, o_u)):
            out[0, :, lanes] = out[0, :, lanes] + grecv[q, n].astype(F32)

    def pf_copy(n):
        step, hh = n % 4, n // 4
        return remote(
            pf.at[0],
            pf.at[(4 - step) % 4],
            pf_s.at[n],
            pf_r.at[(4 - step) % 4],
            device(y + step, h if hh == 0 else 1 - h, z, l, c),
        )

    def t_copy(n):
        target = (device(y, 1 - h, z, l, c), device(y, h, z, 1 - l, c), diagonal)[n]
        return remote(tsend.at[n], trecv.at[n], t_s.at[n], t_r.at[n], target)

    def recv_all(w, shared, copy):
        for k in range(4):
            each_peer(k if shared else 4, lambda cc, k=k: copy(w * 8 + k * 2 + cc).wait_recv())

    for n in range(4):
        chunk(n)
        near_sums(n)
        if n >= 2:
            relay(n - 2)
    other_grads(0)
    relay(2)
    other_grads(1)
    relay(3)
    other_grads(2)
    own_grads()

    @pl.when(active)
    def _():
        po[c] = pb[0]
        for w in range(2):
            recv_all(
                w, w == 0, lambda r: remote(pb.at[0], po.at[r], pb_s.at[0], pb_r.at[r], device(y, 1 - h, z, l, c))
            )
        first, second = named_by(meta[0:1], meta[1:2], expert_column(16))
        sums = [jnp.zeros((1, TOK), F32), jnp.zeros((1, TOK), F32)]
        for r in range(16):
            column = jnp.sum(eye * po[r, 0:1, :], axis=1, keepdims=True)
            row = jnp.sum(p_own[r * CAP : (r + 1) * CAP].astype(F32) * column, axis=0, keepdims=True)
            sums[0] += row * first[r : r + 1]
            sums[1] += row * second[r : r + 1]
        pf[0] = jnp.concatenate(sums + [jnp.zeros((6, TOK), F32)], axis=0)
        for n in range(1, 8):
            pf_copy(n).start()

    for n in range(4):
        back(n)
    other_grads(3)

    @pl.when(active)
    def _():
        for w in range(2):
            into = pl.ds(pl.multiple_of((w * 8 + c) * CAP, CAP), CAP)
            down[:, into] = dback[:, w * 4 * CAP : w * 4 * CAP + CAP]
            recv_all(
                w,
                True,
                lambda r: remote(
                    dback.at[:, pl.ds(0, CAP)],
                    down.at[:, pl.ds(r * CAP, CAP)],
                    rb_s.at[0],
                    rb_r.at[r],
                    device(y, 1 - h, z, l, c),
                ),
            )
            if w == 0:
                tsend[0] = dot(p_back[...], down[1 - h, 0:ROWS]).astype(BF16)
                t_copy(0).start()
                o_tok[...] = dot(p_back[...], down[h, 0:ROWS])
            else:
                tsend[1] = dot(p_oth_back[...], down[h, ROWS : 2 * ROWS]).astype(BF16)
                t_copy(1).start()
                tsend[2] = dot(p_oth_back[...], down[1 - h, ROWS : 2 * ROWS]).astype(BF16)
                t_copy(2).start()
        add_down()
        add_gate_up(0)
        add_gate_up(1)
        t_copy(1).wait_recv()
        o_tok[...] = o_tok[...] + trecv[1].astype(F32)

    @pl.when(idle)
    def _():
        add_down()
        add_gate_up(0)
        add_gate_up(1)
        t_copy(0).wait_recv()
        t_copy(2).wait_recv()
        o_tok[...] = trecv[0].astype(F32) + trecv[2].astype(F32)
        pf_copy(4).wait_recv()

    for n in (1, 2, 3):
        remote(pf.at[0], pf.at[n], pf_s.at[n], pf_r.at[n], device(y + n, h, z, l, c)).wait_recv()
    o_prob[...] = (pf[0] + pf[1] + pf[2] + pf[3])[0:2]

    for q in (2, 3):
        add_gate_up(q)

    @pl.when(active)
    def _():
        each_meta(lambda copy: copy.wait_send())
        for w in range(2):
            for q in range(3 - w):
                for k in range(4):
                    each_peer(k, lambda cc, w=w, k=k, q=q: d_copy(w, k, cc, q).wait_send())
        for n in range(1, 8):
            pf_copy(n).wait_send()
        for n in range(3):
            t_copy(n).wait_send()

    for n in range(3):
        w_copy(n).wait_send()
    for k in range(4):
        for up in range(2):
            f_copy(k, up, base + 1).wait_send()
            for i in range(2):
                e_copy(k, i, up, y).wait_send()
                v_copy(k, i, up, (y + 1) % 4).wait_send()
    for s in range(8):

        each_owner(s, lambda s=s: pb_copy(s).wait_send())
        each_column(s, lambda s=s: rb_copy(s).wait_send())
    for n in range(4):
        for side in range(2):
            far_copy(n, side).wait_send()
            near_copy(n, side).wait_send()
            chain_copy(n, side).wait_send()
    gd_copy().wait_send()
    for q in range(4):
        g_copy(q).wait_send()


def copy_out(*refs):
    copies = [pltpu.make_async_copy(refs[n], refs[5 + n], refs[10].at[n]) for n in range(5)]
    for copy in copies:
        copy.start()
    for copy in copies:
        copy.wait()


def in_hbm(value):
    return pltpu.with_memory_space_constraint(value, pltpu.HBM)


def on_device(tokens, out_grad, expert_ids, gate_probs, w_gate, w_up, w_down):
    dma = pltpu.SemaphoreType.DMA
    hbm = pl.BlockSpec(memory_space=pltpu.HBM)
    vmem = pl.BlockSpec(memory_space=pltpu.VMEM)
    outs = pl.pallas_call(
        kernel,
        out_shape=(
            jax.ShapeDtypeStruct((TOK, 256), F32),
            jax.ShapeDtypeStruct((2, TOK), F32),
            jax.ShapeDtypeStruct((1, FF, D), F32),
            jax.ShapeDtypeStruct((1, FF, D), F32),
            jax.ShapeDtypeStruct((1, FF, D), F32),
        ),
        in_specs=[hbm, hbm, vmem, vmem, hbm, hbm, hbm],
        out_specs=(vmem,) * 5,
        scratch_shapes=[
            pltpu.VMEM((8, TOK), F32),
            pltpu.VMEM((8, 8, TOK), F32),
            pltpu.VMEM((3, TOK, 2 * Q), BF16),
            pltpu.VMEM((TOK, 2 * Q), BF16),
            pltpu.VMEM((3, ROWS, 2 * Q), BF16),
            pltpu.VMEM((2, ROWS, Q), BF16),
            pltpu.VMEM((4, ROWS, 2 * Q), BF16),
            pltpu.VMEM((2, 256, D), BF16),
            pltpu.VMEM((2, 128, D), BF16),
            pltpu.VMEM((TOK, TOK), BF16),
            pltpu.VMEM((16 * CAP, TOK), BF16),
            pltpu.VMEM((TOK, ROWS), BF16),
            pltpu.VMEM((TOK, ROWS), BF16),
            pltpu.VMEM((8 * CAP, TOK), BF16),
            pltpu.VMEM((ROWS, 128), F32),
            pltpu.VMEM((2, ROWS, 256), F32),
            pltpu.VMEM((2, ROWS, 128), F32),
            pltpu.VMEM((2, ROWS, 256), BF16),
            pltpu.VMEM((2, 256, ROWS), BF16),
            pltpu.VMEM((2, 128, ROWS), BF16),
            pltpu.VMEM((ROWS, 128), F32),
            pltpu.VMEM((4, ROWS, Q), BF16),
            pltpu.VMEM((4, ROWS, Q), F32),
            pltpu.VMEM((4, 2, ROWS, 256), BF16),
            pltpu.VMEM((2, ROWS, 256), BF16),
            pltpu.VMEM((2, ROWS, 256), BF16),
            pltpu.VMEM((2, ROWS, 256), BF16),
            pltpu.VMEM((2, ROWS, 256), BF16),
            pltpu.VMEM((2, ROWS, 256), BF16),
            pltpu.VMEM((2, 16 * CAP, 256), BF16),
            pltpu.VMEM((8, 8, 128), F32),
            pltpu.VMEM((16, 8, 128), F32),
            pltpu.VMEM((4, 8, TOK), F32),
            pltpu.VMEM((FF, D), BF16),
            pltpu.VMEM((FF, D), BF16),
            pltpu.VMEM((4, 2, FF, Q), BF16),
            pltpu.VMEM((4, 2, FF, Q), BF16),
            pltpu.VMEM((3, TOK, 256), BF16),
            pltpu.VMEM((3, TOK, 256), BF16),
            dma((9,)),
            dma((16,)),
            dma((8,)),
            dma((2,)),
            dma((2,)),
            dma((3,)),
            dma((3,)),
            dma((48,)),
            dma((24,)),
            dma((8,)),
            dma((8,)),
            dma((16,)),
            dma((16,)),
            dma((16,)),
            dma((16,)),
            dma((8,)),
            dma((8,)),
            dma((8,)),
            dma((8,)),
            dma((8,)),
            dma((8,)),
            dma((8,)),
            dma((16,)),
            dma((8,)),
            dma((16,)),
            dma((1,)),
            dma((1,)),
            dma((4,)),
            dma((4,)),
            dma((3,)),
            dma((3,)),
            dma((8,)),
            dma((4,)),
        ],
        compiler_params=pltpu.CompilerParams(
            collective_id=0, has_side_effects=True, vmem_limit_bytes=48 << 20
        ),
        name="expert_backward",
    )(
        in_hbm(tokens),
        in_hbm(out_grad),
        expert_ids.T,
        gate_probs.T,
        in_hbm(w_gate),
        in_hbm(w_up),
        in_hbm(w_down),
    )
    token_grad, prob, grad_gate, grad_up, grad_down = pl.pallas_call(
        copy_out,
        out_shape=tuple(jax.ShapeDtypeStruct(v.shape, v.dtype) for v in outs),
        in_specs=[pl.BlockSpec(memory_space=pl.ANY)] * 5,
        out_specs=(pl.BlockSpec(memory_space=pl.ANY),) * 5,
        scratch_shapes=[dma((5,))],
        compiler_params=pltpu.CompilerParams(vmem_limit_bytes=1 << 20),
        name="copy_out",
    )(*outs)
    return token_grad, prob.T, grad_gate, grad_up, grad_down


def solution(mesh):
    in_specs = (
        P("expert", None),
        P("expert", None),
        P("expert", None),
        P("expert", None),
        P("expert", "dp", None),
        P("expert", "dp", None),
        P("expert", "dp", None),
    )
    out_specs = (
        P("expert", "dp"),
        P("expert", None),
        P("expert", "dp", None),
        P("expert", "dp", None),
        P("expert", "dp", None),
    )
    return jax.shard_map(
        on_device, mesh=mesh, in_specs=in_specs, out_specs=out_specs, check_vma=False
    )
```

```python
import jax
import jax.numpy as jnp
from jax import lax
from jax.experimental import pallas as pl
from jax.experimental.pallas import tpu as pltpu
from jax.sharding import PartitionSpec as P

MESH = pl.DeviceIdType.MESH
F32 = jnp.float32
BF16 = jnp.bfloat16

D = 2048
FF = 96
TOK = 256
CAP = 64
Q = 512
ROWS = 8 * CAP
HALF = ROWS // 2


def dot(a, b):
    return jnp.dot(a, b, preferred_element_type=F32)


def dot_nt(a, b):
    return lax.dot_general(a, b, (((1,), (1,)), ((), ())), preferred_element_type=F32)


def dot_tn(a, b):
    return lax.dot_general(a, b, (((0,), (0,)), ((), ())), preferred_element_type=F32)


def kernel(
    tok,
    dy,
    ids,
    prob,
    wg,
    wu,
    wd,
    o_tok,
    o_prob,
    o_g,
    o_u,
    o_d,
    meta,
    mb,
    xo,
    raw,
    stage,
    stage_oth,
    slots,
    wgu,
    wdn,
    upper,
    p_own,
    p_back,
    p_oth_back,
    p_oth,
    pcol,
    pre,
    bk,
    ga,
    ga_t,
    hl_t,
    psum,
    scaled,
    dacc,
    dsend,
    far,
    near,
    csend,
    chain,
    dback,
    down,
    pb,
    po,
    pf,
    gd_send,
    gd_recv,
    gsend,
    grecv,
    tsend,
    trecv,
    l_sem,
    m_s,
    m_r,
    raw_s,
    raw_r,
    w_s,
    w_r,
    d_s,
    d_r,
    f_s,
    f_r,
    e_s,
    e_r,
    v_s,
    v_r,
    far_s,
    far_r,
    near_s,
    near_r,
    ch_s,
    ch_r,
    pb_s,
    pb_r,
    rb_s,
    rb_r,
    gd_s,
    gd_r,
    g_s,
    g_r,
    t_s,
    t_r,
    pf_s,
    pf_r,
):
    dp = lax.axis_index("dp")
    ex = lax.axis_index("expert")
    y, h = dp // 2, dp % 2
    z, l, c = ex // 4, (ex // 2) % 2, ex % 2
    active = c == h
    idle = jnp.logical_not(active)
    base = (y % 2) * 2

    def device(yy, hh, zz, ll, cc):
        return (((yy + 4) % 4) * 2 + hh, ((zz + 4) % 4) * 4 + ll * 2 + cc)

    def remote(src, dst, send, recv, target):
        return pltpu.make_async_remote_copy(
            src_ref=src,
            dst_ref=dst,
            send_sem=send,
            recv_sem=recv,
            device_id=target,
            device_id_type=MESH,
        )

    def other(w):
        return l if w == 0 else 1 - l

    diagonal = device(y, 1 - h, z, 1 - l, c)

    barrier = pltpu.get_barrier_semaphore()
    for n in range(1, 16):
        pl.semaphore_signal(barrier, inc=1, device_id=(dp, (ex + n) % 16), device_id_type=MESH)
    for n in range(1, 8):
        pl.semaphore_signal(barrier, inc=1, device_id=((dp + n) % 8, ex), device_id_type=MESH)
    pl.semaphore_signal(barrier, inc=1, device_id=diagonal, device_id_type=MESH)

    local = [
        pltpu.make_async_copy(wg.at[0], wgu.at[0, pl.ds(0, FF)], l_sem.at[0]),
        pltpu.make_async_copy(wu.at[0], wgu.at[0, pl.ds(128, FF)], l_sem.at[1]),
        pltpu.make_async_copy(wd.at[0], wdn.at[0, pl.ds(0, FF)], l_sem.at[2]),
    ]

    def own_quarter(q):
        return (base + q) % 4

    def quarter_of(ref, q):
        return ref.at[:, pl.ds(pl.multiple_of(own_quarter(q) * Q, Q), Q)]

    own_copies = [
        pltpu.make_async_copy(quarter_of(ref, q), xo.at[q, :, pl.ds(i * Q, Q)], l_sem.at[3 + 2 * q + i])
        for q in (1, 0, 2)
        for i, ref in enumerate((tok, dy))
    ]

    @pl.when(active)
    def _():
        for copy in own_copies:
            copy.start()

    for copy in local:
        copy.start()
    meta[...] = jnp.concatenate(
        [ids[...].astype(F32), prob[...].astype(F32), jnp.zeros((4, TOK), F32)], axis=0
    )
    zeros = jnp.zeros((128 - FF, D), BF16)
    for j in range(2):
        wgu[j, FF:128] = zeros
        wgu[j, 128 + FF : 256] = zeros
        wdn[j, FF:128] = zeros
    upper[...] = (
        lax.broadcasted_iota(jnp.int32, (TOK, TOK), 0) < lax.broadcasted_iota(jnp.int32, (TOK, TOK), 1)
    ).astype(F32).astype(BF16)
    slot_iota = lax.broadcasted_iota(jnp.int32, (CAP, TOK), 0).astype(F32)
    eye = (
        lax.broadcasted_iota(jnp.int32, (CAP, 128), 0) == lax.broadcasted_iota(jnp.int32, (CAP, 128), 1)
    ).astype(F32)

    def targets(named):
        before = dot(named.astype(BF16), upper[...])
        return jnp.where(named > 0, before, -1.0)

    def one_hot(target_row):
        return (slot_iota == target_row).astype(F32)

    def named_by(ids0, ids1, experts):
        return (ids0 == experts).astype(F32), (ids1 == experts).astype(F32)

    def expert_column(count):
        r = lax.broadcasted_iota(jnp.int32, (count, 1), 0)
        return (4 * ((z + (r // 2) % 4) % 4) + 2 * ((l + r // 8) % 2) + r % 2).astype(F32)

    @pl.when(active)
    def _():
        mb[0] = meta[...]
        first, second = named_by(meta[0:1], meta[1:2], expert_column(16))
        where = targets(first + second)
        for r in range(16):
            p_own[r * CAP : (r + 1) * CAP] = one_hot(where[r : r + 1]).astype(BF16)

    pl.semaphore_wait(barrier, 23)

    def raw_copy(i):
        return remote(
            (tok, dy)[i].at[:, pl.ds(pl.multiple_of(y * Q, Q), Q)],
            raw.at[:, pl.ds(i * Q, Q)],
            raw_s.at[i],
            raw_r.at[i],
            device(y, h, z, 1 - l, c) if i == 0 else diagonal,
        )

    def meta_copy(w, k, cc):
        n = (w * 4 + k) * 2
        return remote(
            meta, mb.at[w * 4 + k], m_s.at[n + cc], m_r.at[w * 4 + k], device(y, h, z + k, other(w), cc)
        )

    def w_copy(n):
        src = (wg, wu, wd)[n]
        dst = (wgu.at[1, pl.ds(0, FF)], wgu.at[1, pl.ds(128, FF)], wdn.at[1, pl.ds(0, FF)])[n]
        return remote(src.at[0], dst, w_s.at[n], w_r.at[n], device(y, 1 - h, z, l, c))

    def each_peer(k, f):
        for cc in range(2):
            if k == 0:
                pl.when(cc != c)(lambda cc=cc: f(cc))
            else:
                f(cc)

    def each_meta(f):
        for w in range(2):
            for k in range(4):
                each_peer(k if w == 0 else 4, lambda cc, w=w, k=k: f(meta_copy(w, k, cc)))

    order = (1, 3, 2)

    def d_copy(w, k, cc, q):
        n = w * 24 + (k * 2 + cc) * 3 + q
        m = w * 12 + k * 3 + q
        rows = pl.ds((k * 2 + cc) * CAP, CAP)
        into = pl.ds((w * 4 + k) * CAP, CAP)
        return remote(
            stage.at[q, rows] if w == 0 else stage_oth.at[q, rows],
            slots.at[own_quarter(q), into] if w == 0 else slots.at[y, into, pl.ds(q * Q, Q)],
            d_s.at[n],
            d_r.at[m],
            device(y, h, z + k, l, cc),
        )

    def f_copy(k, up, quarter):
        n = 2 * k + up
        rows = slots.at[quarter, pl.ds(k * CAP + 32 * up, 32)]
        return remote(rows, rows, f_s.at[n], f_r.at[n], device(y + (1 if up else -1), h, z, l, c))

    def e_copy(k, i, up, quarter):
        n = (2 * k + i) * 2 + up
        rows = slots.at[quarter, pl.ds((4 + k) * CAP, CAP), pl.ds(i * Q, Q)]
        return remote(rows, rows, e_s.at[n], e_r.at[n], device(y + (1 if up else -1), h, z, l, c))

    def v_copy(k, i, up, quarter):
        n = (2 * k + i) * 2 + up
        rows = slots.at[quarter, pl.ds((4 + k) * CAP + 32 * up, 32), pl.ds(i * Q, Q)]
        return remote(rows, rows, v_s.at[n], v_r.at[n], device(y + (1 if up else -1), h, z, l, c))

    everyone = (0,) + order

    def forward(which):
        for k in which:
            d_copy(0, k, 0, 1).wait_recv()
            for up in range(2):
                f_copy(k, up, base + 1).start()

    def spread(i, which):
        for k in which:
            d_copy(1, k, 0, i).wait_recv()
            for up in range(2):
                e_copy(k, i, up, y).start()

    def pass_on(i):
        for k in everyone:
            for up in range(2):
                quarter = (y + (3 if up else 1)) % 4
                e_copy(k, i, up, quarter).wait_recv()
                v_copy(k, i, up, quarter).start()

    def send_out(w, q, which):
        for k in which:
            each_peer(k, lambda cc, k=k: d_copy(w, k, cc, q).start())

    mine_rows = pl.ds(pl.multiple_of(c * CAP, CAP), CAP)

    def other_block(i):
        raw_copy(i).wait_recv()
        lanes = slice(i * Q, (i + 1) * Q)
        stage_oth[i] = dot(p_oth[...], raw[:, lanes]).astype(BF16)
        send_out(1, i, order + (0,))
        slots[y, 4 * CAP : 5 * CAP, lanes] = stage_oth[i, mine_rows]
        for up in range(2):
            e_copy(0, i, up, y).start()

    def own_block(q):
        stage[q] = dot(p_own[0:ROWS, :], xo[q]).astype(BF16)
        slots[own_quarter(q), 0:CAP] = stage[q, mine_rows]

    @pl.when(active)
    def _():
        raw_copy(0).start()
        each_meta(lambda copy: copy.start())
        for copy in own_copies:
            copy.wait()
        own_block(1)
        send_out(0, 1, order + (0,))
        for up in range(2):
            f_copy(0, up, base + 1).start()
        own_block(0)
        own_block(2)
        meta_copy(1, 0, 0).wait_recv()
        theirs = mb[4]
        first, second = named_by(theirs[0:1], theirs[1:2], expert_column(8))
        where = targets(first + second)
        for r in range(8):
            p_oth[r * CAP : (r + 1) * CAP] = one_hot(where[r : r + 1]).astype(BF16)
        other_block(0)
        other_block(1)
        raw_copy(0).wait_send()
        for n in range(2):
            w_copy(n).start()
        forward(order)

    @pl.when(idle)
    def _():
        raw_copy(1).start()
        raw_copy(1).wait_send()
        for n in range(2):
            w_copy(n).start()
        forward((0,))
        spread(0, (0,))
        forward(order)
        spread(1, (0,))

    spread(0, order)

    @pl.when(active)
    def _():
        for q in (0, 2):
            send_out(0, q, order + (0,))

    spread(1, order)
    w_copy(2).start()
    pass_on(0)

    @pl.when(idle)
    def _():
        meta_copy(0, 0, 0).wait_recv()
        meta_copy(1, 0, 0).wait_recv()

    for s in (1, 2, 3, 5, 6, 7):
        meta_copy(s // 4, s % 4, 0).wait_recv()
    mine = jnp.full((1, 1), ex, jnp.int32).astype(F32)
    firsts, seconds = named_by(mb[:, 0, :], mb[:, 1, :], mine)
    where = targets(firsts + seconds)
    weight = firsts * mb[:, 2, :] + seconds * mb[:, 3, :]
    for s in range(8):
        chosen = one_hot(where[s : s + 1]) * weight[s : s + 1]
        column = jnp.sum(chosen, axis=1, keepdims=True)
        pcol[s * CAP : (s + 1) * CAP] = jnp.broadcast_to(column, (CAP, 128))

    pass_on(1)

    for copy in local:
        copy.wait()

    def inward_gu(j, w):
        rows = slice(w * HALF, (w + 1) * HALF)
        acc = jnp.zeros((HALF, 256), F32)
        for q in range(4):
            acc += dot_nt(slots[q, rows, 0:Q], wgu[j, :, q * Q : (q + 1) * Q])
        pre[j, rows] = acc

    def inward_d(j, w):
        rows = slice(w * HALF, (w + 1) * HALF)
        acc = jnp.zeros((HALF, 128), F32)
        for q in range(4):
            acc += dot_nt(slots[q, rows, Q : 2 * Q], wdn[j, :, q * Q : (q + 1) * Q])
        bk[j, rows] = acc

    def hidden_of(j, rows):
        gate = pre[j, rows, 0:128]
        up = pre[j, rows, 128:256]
        sig = jax.nn.sigmoid(gate)
        act = gate * sig
        return gate, up, sig, act, act * up

    def hidden_grads(j, rows):
        gate, up, sig, act, hidden = hidden_of(j, rows)
        backed = bk[j, rows]
        back = backed * pcol[rows]
        g_gate = back * up * sig * (1.0 + gate * (1.0 - sig))
        g_up = back * act
        ga[j, rows, 0:128] = g_gate.astype(BF16)
        ga[j, rows, 128:256] = g_up.astype(BF16)
        ga_t[j, 0:128, rows] = g_gate.T.astype(BF16)
        ga_t[j, 128:256, rows] = g_up.T.astype(BF16)
        return hidden, hidden * backed

    chunks = [slice(n * 128, n * 128 + 128) for n in range(4)]

    for w in range(2):
        if w == 0:
            pl.when(idle)(lambda: [d_copy(0, 0, 0, q).wait_recv() for q in (0, 2)][0])
            for k in order:
                for q in (0, 2):
                    d_copy(0, k, 0, q).wait_recv()
            for k in everyone:
                for up in range(2):
                    f_copy(k, up, 3 - base).wait_recv()
        else:
            for k in everyone:
                for i in range(2):
                    for up in range(2):
                        v_copy(k, i, up, (y + 2) % 4).wait_recv()
        rows = slice(w * HALF, (w + 1) * HALF)
        for q in range(4):
            scaled[q, rows] = (slots[q, rows, Q : 2 * Q].astype(F32) * pcol[rows, 0:1]).astype(BF16)
        inward_gu(0, w)
        inward_d(0, w)
        for part in chunks[2 * w : 2 * w + 2]:
            hidden, terms = hidden_grads(0, part)
            hl_t[0, :, part] = hidden.T.astype(BF16)
            psum[part] = terms
        for q in range(4):
            dacc[q, rows] = dot(ga[0, rows], wgu[0, :, q * Q : (q + 1) * Q])
        if w == 0:
            for n in range(2):
                w_copy(n).wait_recv()
        inward_gu(1, w)
        for part in chunks[2 * w : 2 * w + 2]:
            hl_t[1, :, part] = hidden_of(1, part)[4].T.astype(BF16)

    def gd_copy():
        return remote(gd_send, gd_recv, gd_s.at[0], gd_r.at[0], device(y, 1 - h, z, l, c))

    def g_copy(q):
        return remote(gsend.at[q], grecv.at[q], g_s.at[q], g_r.at[q], device(y, 1 - h, z, l, c))

    for q in range(4):
        gd_send[:, q * Q : (q + 1) * Q] = dot(hl_t[1], scaled[q]).astype(BF16)[0:FF]
    w_copy(2).wait_recv()
    gd_copy().start()

    def to(step):
        return device(y + step, h, z, l, c)

    def part_of(step, side, n):
        return dsend.at[(y + step + 4) % 4, side, pl.ds(n * 128, 128)]

    def rows_of(ref, side, n):
        return ref.at[side, pl.ds(n * 128, 128)]

    def far_copy(n, side):
        i = 2 * n + side
        return remote(
            part_of(2, side, n), rows_of(far, side, n), far_s.at[i], far_r.at[i], to(-1 if side == 0 else 1)
        )

    def near_copy(n, side):
        i = 2 * n + side
        step = 1 if side == 0 else -1
        return remote(part_of(step, side, n), rows_of(near, side, n), near_s.at[i], near_r.at[i], to(step))

    def chain_copy(n, side):
        i = 2 * n + side
        return remote(
            rows_of(csend, side, n),
            rows_of(chain, side, n),
            ch_s.at[i],
            ch_r.at[i],
            to(-1 if side == 0 else 1),
        )

    def pb_copy(s):
        w, k = s // 4, s % 4
        r = w * 8 + k * 2 + c
        return remote(pb.at[s], po.at[r], pb_s.at[s], pb_r.at[r], device(y, h, z - k, other(w), h))

    def each_owner(s, f):
        if s == 0:
            pl.when(idle)(f)
        else:
            f()

    def relay(n):
        for side in range(2):
            far_copy(n, side).wait_recv()
            step = -1 if side == 0 else 1
            rows = slice(n * 128, n * 128 + 128)
            total = far[side, rows].astype(F32) + dsend[(y + step + 4) % 4, side, rows].astype(F32)
            csend[side, rows] = total.astype(BF16)
            chain_copy(n, side).start()

    def chunk(n):
        part = chunks[n]
        if n % 2 == 0:
            inward_d(1, n // 2)
        terms = hidden_grads(1, part)[1] + psum[part]
        column = jnp.sum(terms, axis=1, keepdims=True)
        for i in range(2):
            s = n * 2 + i
            row = jnp.sum(eye * column[i * CAP : (i + 1) * CAP], axis=0, keepdims=True)
            pb[s] = jnp.broadcast_to(row, (8, 128))
        for q in range(4):
            both = dacc[q, part] + dot(ga[1, part], wgu[1, :, q * Q : (q + 1) * Q])
            low = both.astype(BF16)
            dsend[q, 0, part] = low[:, 0:256]
            dsend[q, 1, part] = low[:, 256:512]
        for side in range(2):
            far_copy(n, side).start()
        for i in range(2):
            each_owner(n * 2 + i, lambda s=n * 2 + i: pb_copy(s).start())

    def near_sums(n):
        for side in range(2):
            near_copy(n, side).start()

    def other_grads(q):
        part = dot(ga_t[1], slots[q, :, 0:Q]).astype(BF16)
        gsend[q, 0] = part[0:FF]
        gsend[q, 1] = part[128 : 128 + FF]
        g_copy(q).start()

    def own_grads():
        for q in range(4):
            lanes = slice(q * Q, (q + 1) * Q)
            part = dot(ga_t[0], slots[q, :, 0:Q])
            o_g[0, :, lanes] = part[0:FF]
            o_u[0, :, lanes] = part[128 : 128 + FF]
            o_d[0, :, lanes] = dot(hl_t[0], scaled[q])[0:FF]

        @pl.when(active)
        def _():
            p_back[...] = p_own[0:ROWS].astype(F32).T.astype(BF16)
            p_oth_back[...] = p_oth[...].astype(F32).T.astype(BF16)

    def rb_copy(s):
        w, k = s // 4, s % 4
        r = w * 8 + k * 2 + c
        return remote(
            dback.at[:, pl.ds(s * CAP, CAP)],
            down.at[:, pl.ds(pl.multiple_of(r * CAP, CAP), CAP)],
            rb_s.at[s],
            rb_r.at[r],
            device(y, h, z - k, l, h),
        )

    def each_column(s, f):
        if s % 4 == 0:
            pl.when(idle)(f)
        else:
            f()

    def back(n):
        part = chunks[n]
        for side in range(2):
            near_copy(n, side).wait_recv()
            chain_copy(n, side).wait_recv()
            total = dsend[y, side, part].astype(F32) + near[side, part].astype(F32)
            dback[side, part] = (total + chain[side, part].astype(F32)).astype(BF16)
        for i in range(2):
            each_column(n * 2 + i, lambda s=n * 2 + i: rb_copy(s).start())

    def add_down():
        gd_copy().wait_recv()
        o_d[0] = o_d[0] + gd_recv[...].astype(F32)

    def add_gate_up(q):
        g_copy(q).wait_recv()
        lanes = slice(q * Q, (q + 1) * Q)
        for n, out in enumerate((o_g, o_u)):
            out[0, :, lanes] = out[0, :, lanes] + grecv[q, n].astype(F32)

    def pf_copy(n):
        step, hh = n % 4, n // 4
        return remote(
            pf.at[0],
            pf.at[(4 - step) % 4],
            pf_s.at[n],
            pf_r.at[(4 - step) % 4],
            device(y + step, h if hh == 0 else 1 - h, z, l, c),
        )

    def t_copy(n):
        target = (device(y, 1 - h, z, l, c), device(y, h, z, 1 - l, c), diagonal)[n]
        return remote(tsend.at[n], trecv.at[n], t_s.at[n], t_r.at[n], target)

    def recv_all(w, shared, copy):
        for k in range(4):
            each_peer(k if shared else 4, lambda cc, k=k: copy(w * 8 + k * 2 + cc).wait_recv())

    for n in range(4):
        chunk(n)
        near_sums(n)
        if n >= 2:
            relay(n - 2)
    other_grads(0)
    relay(2)
    other_grads(1)
    relay(3)
    other_grads(2)
    own_grads()

    @pl.when(active)
    def _():
        po[c] = pb[0]
        for w in range(2):
            recv_all(
                w, w == 0, lambda r: remote(pb.at[0], po.at[r], pb_s.at[0], pb_r.at[r], device(y, 1 - h, z, l, c))
            )
        first, second = named_by(meta[0:1], meta[1:2], expert_column(16))
        sums = [jnp.zeros((1, TOK), F32), jnp.zeros((1, TOK), F32)]
        for r in range(16):
            column = jnp.sum(eye * po[r, 0:1, :], axis=1, keepdims=True)
            row = jnp.sum(p_own[r * CAP : (r + 1) * CAP].astype(F32) * column, axis=0, keepdims=True)
            sums[0] += row * first[r : r + 1]
            sums[1] += row * second[r : r + 1]
        pf[0] = jnp.concatenate(sums + [jnp.zeros((6, TOK), F32)], axis=0)
        for n in range(1, 8):
            pf_copy(n).start()

    for n in range(4):
        back(n)
    other_grads(3)

    @pl.when(active)
    def _():
        for w in range(2):
            into = pl.ds(pl.multiple_of((w * 8 + c) * CAP, CAP), CAP)
            down[:, into] = dback[:, w * 4 * CAP : w * 4 * CAP + CAP]
            recv_all(
                w,
                True,
                lambda r: remote(
                    dback.at[:, pl.ds(0, CAP)],
                    down.at[:, pl.ds(r * CAP, CAP)],
                    rb_s.at[0],
                    rb_r.at[r],
                    device(y, 1 - h, z, l, c),
                ),
            )
            if w == 0:
                tsend[0] = dot(p_back[...], down[1 - h, 0:ROWS]).astype(BF16)
                t_copy(0).start()
                o_tok[...] = dot(p_back[...], down[h, 0:ROWS])
            else:
                tsend[1] = dot(p_oth_back[...], down[h, ROWS : 2 * ROWS]).astype(BF16)
                t_copy(1).start()
                tsend[2] = dot(p_oth_back[...], down[1 - h, ROWS : 2 * ROWS]).astype(BF16)
                t_copy(2).start()
        add_down()
        add_gate_up(0)
        add_gate_up(1)
        t_copy(1).wait_recv()
        o_tok[...] = o_tok[...] + trecv[1].astype(F32)

    @pl.when(idle)
    def _():
        add_down()
        add_gate_up(0)
        add_gate_up(1)
        t_copy(0).wait_recv()
        t_copy(2).wait_recv()
        o_tok[...] = trecv[0].astype(F32) + trecv[2].astype(F32)
        pf_copy(4).wait_recv()

    for n in (1, 2, 3):
        remote(pf.at[0], pf.at[n], pf_s.at[n], pf_r.at[n], device(y + n, h, z, l, c)).wait_recv()
    o_prob[...] = (pf[0] + pf[1] + pf[2] + pf[3])[0:2]

    for q in (2, 3):
        add_gate_up(q)

    @pl.when(active)
    def _():
        each_meta(lambda copy: copy.wait_send())
        for w in range(2):
            for q in range(3 - w):
                for k in range(4):
                    each_peer(k, lambda cc, w=w, k=k, q=q: d_copy(w, k, cc, q).wait_send())
        for n in range(1, 8):
            pf_copy(n).wait_send()
        for n in range(3):
            t_copy(n).wait_send()

    for n in range(3):
        w_copy(n).wait_send()
    for k in range(4):
        for up in range(2):
            f_copy(k, up, base + 1).wait_send()
            for i in range(2):
                e_copy(k, i, up, y).wait_send()
                v_copy(k, i, up, (y + 1) % 4).wait_send()
    for s in range(8):

        each_owner(s, lambda s=s: pb_copy(s).wait_send())
        each_column(s, lambda s=s: rb_copy(s).wait_send())
    for n in range(4):
        for side in range(2):
            far_copy(n, side).wait_send()
            near_copy(n, side).wait_send()
            chain_copy(n, side).wait_send()
    gd_copy().wait_send()
    for q in range(4):
        g_copy(q).wait_send()


def copy_out(*refs):
    copies = [pltpu.make_async_copy(refs[n], refs[5 + n], refs[10].at[n]) for n in range(5)]
    for copy in copies:
        copy.start()
    for copy in copies:
        copy.wait()


def in_hbm(value):
    return pltpu.with_memory_space_constraint(value, pltpu.HBM)


def on_device(tokens, out_grad, expert_ids, gate_probs, w_gate, w_up, w_down):
    dma = pltpu.SemaphoreType.DMA
    hbm = pl.BlockSpec(memory_space=pltpu.HBM)
    vmem = pl.BlockSpec(memory_space=pltpu.VMEM)
    outs = pl.pallas_call(
        kernel,
        out_shape=(
            jax.ShapeDtypeStruct((TOK, 256), F32),
            jax.ShapeDtypeStruct((2, TOK), F32),
            jax.ShapeDtypeStruct((1, FF, D), F32),
            jax.ShapeDtypeStruct((1, FF, D), F32),
            jax.ShapeDtypeStruct((1, FF, D), F32),
        ),
        in_specs=[hbm, hbm, vmem, vmem, hbm, hbm, hbm],
        out_specs=(vmem,) * 5,
        scratch_shapes=[
            pltpu.VMEM((8, TOK), F32),
            pltpu.VMEM((8, 8, TOK), F32),
            pltpu.VMEM((3, TOK, 2 * Q), BF16),
            pltpu.VMEM((TOK, 2 * Q), BF16),
            pltpu.VMEM((3, ROWS, 2 * Q), BF16),
            pltpu.VMEM((2, ROWS, Q), BF16),
            pltpu.VMEM((4, ROWS, 2 * Q), BF16),
            pltpu.VMEM((2, 256, D), BF16),
            pltpu.VMEM((2, 128, D), BF16),
            pltpu.VMEM((TOK, TOK), BF16),
            pltpu.VMEM((16 * CAP, TOK), BF16),
            pltpu.VMEM((TOK, ROWS), BF16),
            pltpu.VMEM((TOK, ROWS), BF16),
            pltpu.VMEM((8 * CAP, TOK), BF16),
            pltpu.VMEM((ROWS, 128), F32),
            pltpu.VMEM((2, ROWS, 256), F32),
            pltpu.VMEM((2, ROWS, 128), F32),
            pltpu.VMEM((2, ROWS, 256), BF16),
            pltpu.VMEM((2, 256, ROWS), BF16),
            pltpu.VMEM((2, 128, ROWS), BF16),
            pltpu.VMEM((ROWS, 128), F32),
            pltpu.VMEM((4, ROWS, Q), BF16),
            pltpu.VMEM((4, ROWS, Q), F32),
            pltpu.VMEM((4, 2, ROWS, 256), BF16),
            pltpu.VMEM((2, ROWS, 256), BF16),
            pltpu.VMEM((2, ROWS, 256), BF16),
            pltpu.VMEM((2, ROWS, 256), BF16),
            pltpu.VMEM((2, ROWS, 256), BF16),
            pltpu.VMEM((2, ROWS, 256), BF16),
            pltpu.VMEM((2, 16 * CAP, 256), BF16),
            pltpu.VMEM((8, 8, 128), F32),
            pltpu.VMEM((16, 8, 128), F32),
            pltpu.VMEM((4, 8, TOK), F32),
            pltpu.VMEM((FF, D), BF16),
            pltpu.VMEM((FF, D), BF16),
            pltpu.VMEM((4, 2, FF, Q), BF16),
            pltpu.VMEM((4, 2, FF, Q), BF16),
            pltpu.VMEM((3, TOK, 256), BF16),
            pltpu.VMEM((3, TOK, 256), BF16),
            dma((9,)),
            dma((16,)),
            dma((8,)),
            dma((2,)),
            dma((2,)),
            dma((3,)),
            dma((3,)),
            dma((48,)),
            dma((24,)),
            dma((8,)),
            dma((8,)),
            dma((16,)),
            dma((16,)),
            dma((16,)),
            dma((16,)),
            dma((8,)),
            dma((8,)),
            dma((8,)),
            dma((8,)),
            dma((8,)),
            dma((8,)),
            dma((8,)),
            dma((16,)),
            dma((8,)),
            dma((16,)),
            dma((1,)),
            dma((1,)),
            dma((4,)),
            dma((4,)),
            dma((3,)),
            dma((3,)),
            dma((8,)),
            dma((4,)),
        ],
        compiler_params=pltpu.CompilerParams(
            collective_id=0, has_side_effects=True, vmem_limit_bytes=48 << 20
        ),
        name="expert_backward",
    )(
        in_hbm(tokens),
        in_hbm(out_grad),
        expert_ids.T,
        gate_probs.T,
        in_hbm(w_gate),
        in_hbm(w_up),
        in_hbm(w_down),
    )
    token_grad, prob, grad_gate, grad_up, grad_down = pl.pallas_call(
        copy_out,
        out_shape=tuple(jax.ShapeDtypeStruct(v.shape, v.dtype) for v in outs),
        in_specs=[pl.BlockSpec(memory_space=pl.ANY)] * 5,
        out_specs=(pl.BlockSpec(memory_space=pl.ANY),) * 5,
        scratch_shapes=[dma((5,))],
        compiler_params=pltpu.CompilerParams(vmem_limit_bytes=1 << 20),
        name="copy_out",
    )(*outs)
    return token_grad, prob.T, grad_gate, grad_up, grad_down


def solution(mesh):
    in_specs = (
        P("expert", None),
        P("expert", None),
        P("expert", None),
        P("expert", None),
        P("expert", "dp", None),
        P("expert", "dp", None),
        P("expert", "dp", None),
    )
    out_specs = (
        P("expert", "dp"),
        P("expert", None),
        P("expert", "dp", None),
        P("expert", "dp", None),
        P("expert", "dp", None),
    )
    return jax.shard_map(
        on_device, mesh=mesh, in_specs=in_specs, out_specs=out_specs, check_vma=False
    )
```
